256 devices in a mesh: dp: 64 (over x, z, core), mp: 4 (over y).
Axes of the slice: x: 4, y: 4, z: 8, core: 2. Of those that a mesh axis runs over, the one named last changes fastest.
Arguments:
- gradient: bfloat16 [64, 3, 192, 7168], P('dp', None, None, 'mp'), may hold values from -52 to 52
- error_memory: float32 [64, 3, 192, 7168], P('dp', None, None, 'mp'), may hold values from -4 to 4
- right_factor_initial: float32 [3, 32, 7168], P(None, None, 'mp'), may hold values from -6 to 6
Outputs:
- right_factor_next: float32 [3, 32, 7168], P(None, None, 'mp')
- error_next: float32 [64, 3, 192, 7168], P('dp', None, None, 'mp')
The draws below stay inside these ranges and needn't reach their ends.
All inputs are finite; a program needn't handle non-finite values.
Results may differ from the reference program's by a relative error of at most 0.0003.
Values sent between devices are 32-bit elements; how exact they have to be, the bound alone decides.
A program may use at most 64 MiB of HBM per device.

```python
import math
import jax
import jax.numpy as jnp
from jax import lax

D = 7168
RANK = 32
ROWS = 192
BUCKETS = 3
N_DP = 64


def draw_gradient(key, part):
    key = jax.random.fold_in(key, 7)
    keys = jax.random.split(key, 4)
    shared_value = jnp.clip(jax.random.normal(keys[0], (BUCKETS, ROWS, D)), -5.0, 5.0)
    own = jnp.clip(jax.random.normal(keys[1], (N_DP, BUCKETS, ROWS, D)), -5.0, 5.0)
    column_scale = jnp.exp(jax.random.uniform(keys[2], (BUCKETS, 1, D), minval=math.log(0.3), maxval=math.log(3.0)))
    row_scale = jnp.exp(jax.random.uniform(keys[3], (BUCKETS, ROWS, 1), minval=math.log(0.5), maxval=math.log(2.0)))
    return ((shared_value[None] + 0.7 * own) * (column_scale * row_scale)[None]).astype(jnp.bfloat16)


def steps_of(key, shape, cuts, least, high):
    def one(axis_at, parts):
        draws = jax.random.uniform(jax.random.fold_in(jax.random.fold_in(key, 6), axis_at), (parts,), jnp.float32, least / len(cuts), high / len(cuts))
        return jnp.repeat(jnp.exp(draws), shape[axis_at] // parts).reshape((-1,) + (1,) * (len(shape) - axis_at - 1))

    gain = one(*cuts[0])
    for cut in cuts[1:]:
        gain = gain * one(*cut)
    return gain


def normal_values(own_key, shape, width, most, cuts=(), kind=jnp.bfloat16):
    array = width * jax.random.normal(own_key, shape, jnp.float32)
    if cuts:
        array = array * steps_of(own_key, shape, cuts, -0.22, 0.18)
    return jnp.clip(array, -most, most).astype(kind)


def setup_inputs(seed: int = 0) -> dict:
    arg_keys = jax.random.split(jax.random.key(seed), 4)
    return {
        "gradient": draw_gradient(jax.random.fold_in(arg_keys[3], 71), 0),
        "error_memory": normal_values(arg_keys[1], (N_DP, BUCKETS, ROWS, D), 0.3, 4.0, ((0, 64), (3, 4)), jnp.float32),
        "right_factor_initial": normal_values(arg_keys[2], (BUCKETS, RANK, D), 1.0, 6.0, ((2, 4),), jnp.float32),
    }


def orthonormal(left_factor_rows):
    gram_matrix = jnp.einsum('bkr,bjr->bkj', left_factor_rows, left_factor_rows, precision=lax.Precision.HIGHEST)
    factor = jnp.linalg.cholesky(gram_matrix)
    return lax.linalg.triangular_solve(factor, left_factor_rows, left_side=True, lower=True)

def reference(gradient, error_memory, right_factor_initial):
    corrected = gradient.astype(jnp.float32) + error_memory
    averaged_matrix = jnp.sum(corrected, axis=0) * (1.0 / N_DP)
    left_factor_rows = jnp.einsum('ifv,ijv->ifj', right_factor_initial, averaged_matrix, precision=lax.Precision.HIGHEST)
    column_basis = orthonormal(left_factor_rows)
    right_factor_next = jnp.einsum('jfh,jhi->jfi', column_basis, averaged_matrix, precision=lax.Precision.HIGHEST)
    approximation = jnp.einsum('zoq,zoa->zqa', column_basis, right_factor_next, precision=lax.Precision.HIGHEST)
    error_next = corrected - approximation[None]
    return (right_factor_next, error_next)
```

```python
import functools

import jax
import jax.numpy as jnp
from jax import lax
from jax.experimental import pallas as pl
from jax.experimental.pallas import tpu as pltpu
from jax.sharding import PartitionSpec as P

MESH = pl.DeviceIdType.MESH
NX, NY, NZ = 4, 4, 8
BUCKETS, RANK, ROWS = 3, 32, 192
GROUP = NX * NY
PIECE = ROWS // GROUP
XY = [(i, j) for i in range(NX) for j in range(NY) if i or j]
F32, BF16 = jnp.float32, jnp.bfloat16
HIGHEST = lax.Precision.HIGHEST


def place():
    dp = lax.axis_index("dp")
    return dp // (2 * NZ), lax.axis_index("mp"), (dp // 2) % NZ, dp % 2


def device(x, y, z, c):
    return ((x * NZ + z) * 2 + c, y)


def split(value):
    high = value.astype(BF16)
    return high, (value - high.astype(F32)).astype(BF16)


def dot(a, b, dims=((1,), (0,))):
    return lax.dot_general(a, b, (dims, ((), ())), preferred_element_type=F32)


def inverse_factor(gram, lane):
    column = lane % RANK
    row = lax.broadcasted_iota(jnp.int32, (RANK, 128), 0)
    group = lane - column
    z = gram
    done = jnp.zeros((RANK, 128), F32)
    block = 8
    for start in range(0, RANK, block):
        cols = [
            jnp.take_along_axis(z, group + (start + t), axis=1) for t in range(block)
        ]
        for t in range(block):
            k = start + t
            scale = lax.rsqrt(cols[t][k : k + 1, :])
            below = jnp.where(row > k, cols[t] * scale, 0.0)
            pivot = jnp.where(column[k : k + 1] == k, scale, z[k : k + 1, :] * scale)
            done = jnp.where(row == k, pivot, done)
            z = jnp.where(column == k, 0.0, z) - below * pivot
            for u in range(t + 1, block):
                cols[u] = cols[u] - below * (cols[u][k : k + 1, :] * scale)
    return jnp.where(column <= row, done, 0.0)


def reduce_kernel(
    g_hbm, e_hbm, r_hbm, q_hbm, w_ref,
    g_ref, e_ref, r_ref, ch_ref, cl_ref, rr_ref,
    ps, pr, pcs, pcr, pzs, pzr, pg, pf,
    qs, qc, xs, xr, zs, zr, zg, qg,
    in_sem, out_sem,
    pa_s, pa_r, pc_s, pc_r, pz_s, pz_r, pg_s, pg_r,
    s1_s, s1_r, s2_s, s2_r, s3_s, s3_r, s4_s, s4_r, s5_s, s5_r, s6_s, s6_r,
):
    x, y, z, c = place()
    xy_peers = [((x + i) % NX, (y + j) % NY) for i, j in XY]
    x_peers = [(x + i) % NX for i in range(1, NX)]
    z_peers = [(z + i) % NZ for i in range(1, NZ)]
    mine = x * NY + y

    barrier = pltpu.get_barrier_semaphore()
    for px, py in xy_peers:
        pl.semaphore_signal(barrier, inc=1, device_id=device(px, py, z, c), device_id_type=MESH)
    for pz in z_peers:
        pl.semaphore_signal(barrier, inc=1, device_id=device(x, y, pz, c), device_id_type=MESH)
    pl.semaphore_signal(barrier, inc=1, device_id=device(x, y, z, 1 - c), device_id_type=MESH)

    loads = [pltpu.make_async_copy(r_hbm, r_ref, in_sem.at[0])]
    for b in range(BUCKETS):
        loads.append(pltpu.make_async_copy(g_hbm.at[0, b], g_ref.at[b], in_sem.at[1 + 2 * b]))
        loads.append(pltpu.make_async_copy(e_hbm.at[0, b], e_ref.at[b], in_sem.at[2 + 2 * b]))
    for load in loads:
        load.start()

    sends = []

    def send(src, dst, send_sem, recv_sem, where):
        copy = pltpu.make_async_remote_copy(
            src_ref=src, dst_ref=dst, send_sem=send_sem, recv_sem=recv_sem,
            device_id=device(*where), device_id_type=MESH,
        )
        copy.start()
        sends.append(copy)
        return copy

    width = r_ref.shape[2]
    loads[0].wait()
    rr_ref[...] = jnp.zeros_like(rr_ref)
    for b in range(BUCKETS):
        high, low = split(r_ref[b])
        rr_ref[b * RANK : (b + 1) * RANK, :] = high
        rr_ref[128 + b * RANK : 128 + (b + 1) * RANK, :] = low

    lane = lax.broadcasted_iota(jnp.int32, (RANK, 128), 1)
    lane_rows = lax.broadcasted_iota(jnp.int32, (ROWS, 128), 1)
    step = 16
    total = jnp.zeros((ROWS, 128), F32)
    for b in range(BUCKETS):
        loads[1 + 2 * b].wait()
        loads[2 + 2 * b].wait()

        @pl.loop(0, ROWS // step)
        def _(i):
            rows = pl.ds(pl.multiple_of(i * step, step), step)
            high, low = split(g_ref[b, rows, :].astype(F32) + e_ref[b, rows, :])
            ch_ref[b, rows, :] = high
            cl_ref[b, rows, :] = low

        both = dot(ch_ref[b], rr_ref[...], ((1,), (1,)))
        part = both[:, :128] + both[:, 128:] + dot(cl_ref[b], rr_ref[:128, :], ((1,), (1,)))
        total = jnp.where(lane_rows // RANK == b, part, total)
    total = total * (1.0 / 64)
    for i in range(GROUP):
        ps[i] = total[i * PIECE : (i + 1) * PIECE, :]

    pl.semaphore_wait(barrier, len(XY) + NZ)

    copies = [
        send(ps.at[px * NY + py], pr.at[i], pa_s.at[i], pa_r.at[i], (px, py, z, c))
        for i, (px, py) in enumerate(xy_peers)
    ]
    piece = ps[mine]
    for i, copy in enumerate(copies):
        copy.wait_recv()
        piece = piece + pr[i]
    pcs[...] = piece
    copy = send(pcs, pcr, pc_s, pc_r, (x, y, z, 1 - c))
    copy.wait_recv()
    piece = piece + pcr[...]
    pzs[...] = piece
    copies = [
        send(pzs, pzr.at[i], pz_s.at[i], pz_r.at[i], (x, y, pz, c)) for i, pz in enumerate(z_peers)
    ]
    for i, copy in enumerate(copies):
        copy.wait_recv()
        piece = piece + pzr[i]
    pg[mine] = piece
    copies = [
        send(pg.at[mine], pg.at[mine], pg_s.at[i], pg_r.at[i], (px, py, z, c))
        for i, (px, py) in enumerate(xy_peers)
    ]
    for copy in copies:
        copy.wait_recv()
    for i in range(GROUP):
        pf[i * PIECE : (i + 1) * PIECE, :] = pg[i]
    pf[ROWS:, :] = jnp.zeros((256 - ROWS, 128), F32)

    left_t = pf[...]
    left = left_t.T
    gram = lax.dot_general(
        left, left_t, (((1,), (0,)), ((), ())), precision=HIGHEST, preferred_element_type=F32
    )
    packed = jnp.zeros((RANK, 128), F32)
    for b in range(BUCKETS):
        packed = jnp.where(lane // RANK == b, gram[b * RANK : (b + 1) * RANK, :], packed)
    inverse = inverse_factor(packed, lane)
    blocks = [jnp.where(lane // RANK == b, inverse, 0.0) for b in range(BUCKETS)]
    blocks.append(jnp.zeros((RANK, 128), F32))
    basis = lax.dot_general(
        jnp.concatenate(blocks, axis=0), left, (((1,), (0,)), ((), ())),
        precision=HIGHEST, preferred_element_type=F32,
    )[:, :ROWS]
    basis_high, basis_low = split(basis)

    def local_q(b):
        rows = slice(b * RANK, (b + 1) * RANK)
        stacked = jnp.concatenate([basis_high[rows], basis_low[rows]], axis=0)
        half = width // 2
        for start in range(0, width, 256):
            stop = start + 256
            one = dot(stacked, ch_ref[b, :, start:stop])
            value = one[:RANK] + one[RANK:] + dot(basis_high[rows], cl_ref[b, :, start:stop])
            if stop <= half:
                qs[b, 0, :, start:stop] = value
            elif start >= half:
                qs[b, 1, :, start - half : stop - half] = value
            else:
                qs[b, 0, :, start:half] = value[:, : half - start]
                qs[b, 1, :, : stop - half] = value[:, half - start :]

    first, second, third, fourth, fifth, sixth = ({} for _ in range(6))
    tiles = width // 2 // 128

    def send_core(b):
        first[b] = send(qs.at[b, 1 - c], qc.at[b], s1_s.at[b], s1_r.at[b], (x, y, z, 1 - c))

    def send_x(b):
        first[b].wait_recv()
        for t in range(4):
            xs[b, t] = qs[b, c, 8 * t : 8 * t + 8, :] + qc[b, 8 * t : 8 * t + 8, :]
        second[b] = [
            send(xs.at[b, px], xr.at[b, i], s2_s.at[b, i], s2_r.at[b, i], (px, y, z, c))
            for i, px in enumerate(x_peers)
        ]

    def send_z(b):
        value = xs[b, x]
        for i, copy in enumerate(second[b]):
            copy.wait_recv()
            value = value + xr[b, i]
        for t in range(tiles):
            zs[b, t] = value[:, t * 128 : (t + 1) * 128]
        zs[b, tiles] = jnp.zeros((8, 128), F32)
        third[b] = [
            send(zs.at[b, pz], zr.at[b, i], s3_s.at[b, i], s3_r.at[b, i], (x, y, pz, c))
            for i, pz in enumerate(z_peers)
        ]

    def back_z(b):
        value = zs[b, z]
        for i, copy in enumerate(third[b]):
            copy.wait_recv()
            value = value + zr[b, i]
        zg[b, z] = value * (1.0 / 64)
        fourth[b] = [
            send(zg.at[b, z], zg.at[b, z], s4_s.at[b, i], s4_r.at[b, i], (x, y, pz, c))
            for i, pz in enumerate(z_peers)
        ]

    def back_x(b):
        for copy in fourth[b]:
            copy.wait_recv()
        for t in range(tiles):
            qg[b, c, x, :, t * 128 : (t + 1) * 128] = zg[b, t]
        fifth[b] = [
            send(qg.at[b, c, x], qg.at[b, c, x], s5_s.at[b, i], s5_r.at[b, i], (px, y, z, c))
            for i, px in enumerate(x_peers)
        ]

    def back_core(b):
        for copy in fifth[b]:
            copy.wait_recv()
        sixth[b] = send(qg.at[b, c], qg.at[b, c], s6_s.at[b], s6_r.at[b], (x, y, z, 1 - c))

    local_q(0)
    send_core(0)
    local_q(1)
    send_x(0)
    send_core(1)
    local_q(2)
    send_x(1)
    send_core(2)
    send_x(2)
    for b in range(BUCKETS):
        turned = basis[b * RANK : (b + 1) * RANK].T
        high, low = split(turned)
        w_ref[b] = jnp.concatenate([high, low, high, jnp.zeros((ROWS, RANK), BF16)], axis=1)
    for stage in (send_z, back_z, back_x, back_core):
        for b in range(BUCKETS):
            stage(b)
    outs = []
    for b in range(BUCKETS):
        sixth[b].wait_recv()
        out = pltpu.make_async_copy(qg.at[b], q_hbm.at[b], out_sem.at[b])
        out.start()
        outs.append(out)
    for copy in sends:
        copy.wait_send()
    for out in outs:
        out.wait()


def error_kernel(g_ref, e_ref, w_ref, q_ref, q_out, err_ref):
    half = q_ref.shape[-1]
    for h in range(2):
        q = jnp.concatenate([q_ref[0, h, t] for t in range(4)], axis=0)
        cols = slice(h * half, (h + 1) * half)
        q_out[0, :, cols] = q
        high, low = split(q)
        stacked = jnp.concatenate([high, high, low, jnp.zeros_like(high)], axis=0)
        approx = dot(w_ref[0], stacked)
        err_ref[0, 0, :, cols] = g_ref[0, 0, :, cols].astype(F32) + e_ref[0, 0, :, cols] - approx


def per_device(gradient, error_memory, right_factor_initial):
    width = right_factor_initial.shape[2]
    half = width // 2
    dma = pltpu.SemaphoreType.DMA
    vmem = pltpu.VMEM
    hbm = pl.BlockSpec(memory_space=pl.ANY)
    b3 = BUCKETS
    n_xy, n_x, n_z = len(XY), NX - 1, NZ - 1
    q, w = pl.pallas_call(
        reduce_kernel,
        out_shape=(
            jax.ShapeDtypeStruct((b3, 2, 4, 8, half), F32),
            jax.ShapeDtypeStruct((b3, ROWS, 128), BF16),
        ),
        in_specs=[hbm, hbm, hbm],
        out_specs=(hbm, pl.BlockSpec(memory_space=pltpu.VMEM)),
        scratch_shapes=[
            vmem((b3, ROWS, width), BF16),
            vmem((b3, ROWS, width), F32),
            vmem((b3, RANK, width), F32),
            vmem((b3, ROWS, width), BF16),
            vmem((b3, ROWS, width), BF16),
            vmem((256, width), BF16),
            vmem((GROUP, PIECE, 128), F32),
            vmem((n_xy, PIECE, 128), F32),
            vmem((PIECE, 128), F32),
            vmem((PIECE, 128), F32),
            vmem((PIECE, 128), F32),
            vmem((n_z, PIECE, 128), F32),
            vmem((GROUP, PIECE, 128), F32),
            vmem((256, 128), F32),
            vmem((b3, 2, RANK, half), F32),
            vmem((b3, RANK, half), F32),
            vmem((b3, 4, 8, half), F32),
            vmem((b3, n_x, 8, half), F32),
            vmem((b3, NZ, 8, 128), F32),
            vmem((b3, n_z, 8, 128), F32),
            vmem((b3, NZ, 8, 128), F32),
            vmem((b3, 2, 4, 8, half), F32),
            dma((1 + 2 * b3,)),
            dma((b3,)),
            dma((n_xy,)), dma((n_xy,)),
            dma, dma,
            dma((n_z,)), dma((n_z,)),
            dma((n_xy,)), dma((n_xy,)),
            dma((b3,)), dma((b3,)),
            dma((b3, n_x)), dma((b3, n_x)),
            dma((b3, n_z)), dma((b3, n_z)),
            dma((b3, n_z)), dma((b3, n_z)),
            dma((b3, n_x)), dma((b3, n_x)),
            dma((b3,)), dma((b3,)),
        ],
        compiler_params=pltpu.CompilerParams(
            collective_id=0, has_side_effects=True, vmem_limit_bytes=32 << 20
        ),
        name="reduce_kernel",
    )(gradient, error_memory, right_factor_initial)

    return pl.pallas_call(
        error_kernel,
        grid=(b3,),
        out_shape=(
            jax.ShapeDtypeStruct((b3, RANK, width), F32),
            jax.ShapeDtypeStruct((1, b3, ROWS, width), F32),
        ),
        in_specs=[
            pl.BlockSpec((1, 1, ROWS, width), lambda b: (0, b, 0, 0)),
            pl.BlockSpec((1, 1, ROWS, width), lambda b: (0, b, 0, 0)),
            pl.BlockSpec((1, ROWS, 128), lambda b: (b, 0, 0)),
            pl.BlockSpec((1, 2, 4, 8, half), lambda b: (b, 0, 0, 0, 0)),
        ],
        out_specs=(
            pl.BlockSpec((1, RANK, width), lambda b: (b, 0, 0)),
            pl.BlockSpec((1, 1, ROWS, width), lambda b: (0, b, 0, 0)),
        ),
        compiler_params=pltpu.CompilerParams(vmem_limit_bytes=32 << 20),
        name="error_kernel",
    )(gradient, error_memory, w, q)


def solution(mesh):
    placed = (P("dp", None, None, "mp"), P("dp", None, None, "mp"), P(None, None, "mp"))
    return jax.shard_map(
        per_device,
        mesh=mesh,
        in_specs=placed,
        out_specs=(P(None, None, "mp"), P("dp", None, None, "mp")),
        check_vma=False,
    )
```

```python
import functools

import jax
import jax.numpy as jnp
from jax import lax
from jax.experimental import pallas as pl
from jax.experimental.pallas import tpu as pltpu
from jax.sharding import PartitionSpec as P

MESH = pl.DeviceIdType.MESH
NX, NY, NZ = 4, 4, 8
BUCKETS, RANK, ROWS = 3, 32, 192
GROUP = NX * NY
PIECE = ROWS // GROUP
HOPS = [0, 1, 2, 1]
XY = sorted(
    ((i, j) for i in range(NX) for j in range(NY) if i or j), key=lambda p: -HOPS[p[0]] - HOPS[p[1]]
)
XS = [2, 1, 3]
ZS = [4, 3, 5, 2, 6, 1, 7]
F32, BF16 = jnp.float32, jnp.bfloat16
HIGHEST = lax.Precision.HIGHEST


def place():
    dp = lax.axis_index("dp")
    return dp // (2 * NZ), lax.axis_index("mp"), (dp // 2) % NZ, dp % 2


def device(x, y, z, c):
    return ((x * NZ + z) * 2 + c, y)


def split(value):
    high = value.astype(BF16)
    return high, (value - high.astype(F32)).astype(BF16)


def dot(a, b, dims=((1,), (0,))):
    return lax.dot_general(a, b, (dims, ((), ())), preferred_element_type=F32)


def eliminate(z, done, lane, start, stop):
    column = lane % RANK
    row = lax.broadcasted_iota(jnp.int32, (RANK, 128), 0)
    group = lane - column
    cols = [jnp.take_along_axis(z, group + k, axis=1) for k in range(start, stop)]
    for t in range(stop - start):
        k = start + t
        scale = lax.rsqrt(cols[t][k : k + 1, :])
        below = jnp.where(row > k, cols[t] * scale, 0.0)
        pivot = jnp.where(column[k : k + 1] == k, scale, z[k : k + 1, :] * scale)
        done = jnp.where(row == k, pivot, done)
        z = jnp.where(column == k, 0.0, z) - below * pivot
        for u in range(t + 1, stop - start):
            cols[u] = cols[u] - below * (cols[u][k : k + 1, :] * scale)
    return z, done


def reduce_kernel(
    c_ref, r_ref, q_ref, err_ref,
    ch_ref, cl_ref, rr_ref, w_ref,
    ps, pr, pcs, pcr, zp, pg, pf,
    qs, qc, xs, xr, zs, zr, zg, qg,
    pa_s, pa_r, pc_s, pc_r, pz_s, pz_r, pg_s, pg_r,
    s1_s, s1_r, s2_s, s2_r, s3_s, s3_r, s4_s, s4_r, s5_s, s5_r, s6_s, s6_r,
):
    x, y, z, c = place()
    xy_peers = [((x + i) % NX, (y + j) % NY) for i, j in XY]
    x_peers = [(x + i) % NX for i in XS]
    z_peers = [(z + i) % NZ for i in ZS]
    mine = x * NY + y

    barrier = pltpu.get_barrier_semaphore()
    for px, py in xy_peers:
        pl.semaphore_signal(barrier, inc=1, device_id=device(px, py, z, c), device_id_type=MESH)
    for pz in z_peers:
        pl.semaphore_signal(barrier, inc=1, device_id=device(x, y, pz, c), device_id_type=MESH)
    pl.semaphore_signal(barrier, inc=1, device_id=device(x, y, z, 1 - c), device_id_type=MESH)

    sends = []

    def send(src, dst, send_sem, recv_sem, where):
        copy = pltpu.make_async_remote_copy(
            src_ref=src, dst_ref=dst, send_sem=send_sem, recv_sem=recv_sem,
            device_id=device(*where), device_id_type=MESH,
        )
        copy.start()
        sends.append(copy)
        return copy

    width = r_ref.shape[2]
    rr_ref[...] = jnp.zeros_like(rr_ref)
    for b in range(BUCKETS):
        high, low = split(r_ref[b])
        rr_ref[b * RANK : (b + 1) * RANK, :] = high
        rr_ref[128 + b * RANK : 128 + (b + 1) * RANK, :] = low

    lane = lax.broadcasted_iota(jnp.int32, (RANK, 128), 1)
    lane_rows = lax.broadcasted_iota(jnp.int32, (ROWS, 128), 1)
    step = 256
    total = jnp.zeros((ROWS, 128), F32)
    for b in range(BUCKETS):
        both = jnp.zeros((ROWS, 256), F32)
        rest = jnp.zeros((ROWS, 128), F32)
        for start in range(0, width, step):
            cols = slice(start, start + step)
            value = c_ref[b, :, cols]
            high, low = split(value)
            ch_ref[b, :, cols] = high
            cl_ref[b, :, cols] = low
            both = both + dot(high, rr_ref[:, cols], ((1,), (1,)))
            rest = rest + dot(low, rr_ref[:128, cols], ((1,), (1,)))
        part = both[:, :128] + both[:, 128:] + rest
        total = jnp.where(lane_rows // RANK == b, part, total)
    total = total * (1.0 / 64)
    for i in range(GROUP):
        ps[i] = total[i * PIECE : (i + 1) * PIECE, :]

    pl.semaphore_wait(barrier, len(XY) + NZ)

    copies = [
        send(ps.at[px * NY + py], pr.at[i], pa_s.at[i], pa_r.at[i], (px, py, z, c))
        for i, (px, py) in enumerate(xy_peers)
    ]
    piece = ps[mine]
    for i, copy in enumerate(copies):
        copy.wait_recv()
        piece = piece + pr[i]
    pcs[...] = piece
    copy = send(pcs, pcr, pc_s, pc_r, (x, y, z, 1 - c))
    copy.wait_recv()
    piece = piece + pcr[...]
    zp[z] = piece
    copies = [
        send(zp.at[z], zp.at[z], pz_s.at[i], pz_r.at[i], (x, y, at, c)) for i, at in enumerate(z_peers)
    ]
    for copy in copies:
        copy.wait_recv()
    piece = zp[0]
    for i in range(1, NZ):
        piece = piece + zp[i]
    pg[mine] = piece
    copies = [
        send(pg.at[mine], pg.at[mine], pg_s.at[i], pg_r.at[i], (px, py, z, c))
        for i, (px, py) in enumerate(xy_peers)
    ]
    for copy in copies:
        copy.wait_recv()
    for i in range(GROUP):
        pf[i * PIECE : (i + 1) * PIECE, :] = pg[i]
    pf[ROWS:, :] = jnp.zeros((256 - ROWS, 128), F32)

    left_t = pf[...]
    left = left_t.T
    left_high, left_low = split(left[:, :ROWS])

    def local_t(b):
        rows = slice(b * RANK, (b + 1) * RANK)
        stacked = jnp.concatenate([left_high[rows], left_low[rows]], axis=0)
        half = width // 2
        for start in range(0, width, 256):
            stop = start + 256
            one = dot(stacked, ch_ref[b, :, start:stop])
            value = one[:RANK] + one[RANK:] + dot(left_high[rows], cl_ref[b, :, start:stop])
            if stop <= half:
                qs[b, 0, :, start:stop] = value
            elif start >= half:
                qs[b, 1, :, start - half : stop - half] = value
            else:
                qs[b, 0, :, start:half] = value[:, : half - start]
                qs[b, 1, :, : stop - half] = value[:, half - start :]

    first, second, third, fourth, fifth, sixth = ({} for _ in range(6))
    tiles = width // 2 // 128

    def send_core(b):
        first[b] = send(qs.at[b, 1 - c], qc.at[b], s1_s.at[b], s1_r.at[b], (x, y, z, 1 - c))

    def send_x(b):
        first[b].wait_recv()
        for t in range(4):
            xs[b, t] = qs[b, c, 8 * t : 8 * t + 8, :] + qc[b, 8 * t : 8 * t + 8, :]
        second[b] = [
            send(xs.at[b, px], xr.at[b, i], s2_s.at[b, i], s2_r.at[b, i], (px, y, z, c))
            for i, px in enumerate(x_peers)
        ]

    def send_z(b):
        value = xs[b, x]
        for i, copy in enumerate(second[b]):
            copy.wait_recv()
            value = value + xr[b, i]
        for t in range(tiles):
            zs[b, t] = value[:, t * 128 : (t + 1) * 128]
        zs[b, tiles] = jnp.zeros((8, 128), F32)
        third[b] = [
            send(zs.at[b, pz], zr.at[b, i], s3_s.at[b, i], s3_r.at[b, i], (x, y, pz, c))
            for i, pz in enumerate(z_peers)
        ]

    def back_z(b):
        value = zs[b, z]
        for i, copy in enumerate(third[b]):
            copy.wait_recv()
            value = value + zr[b, i]
        zg[b, z] = value * (1.0 / 64)
        fourth[b] = [
            send(zg.at[b, z], zg.at[b, z], s4_s.at[b, i], s4_r.at[b, i], (x, y, pz, c))
            for i, pz in enumerate(z_peers)
        ]

    def back_x(b):
        for copy in fourth[b]:
            copy.wait_recv()
        for t in range(tiles):
            qg[b, c, x, :, t * 128 : (t + 1) * 128] = zg[b, t]
        fifth[b] = [
            send(qg.at[b, c, x], qg.at[b, c, x], s5_s.at[b, i], s5_r.at[b, i], (px, y, z, c))
            for i, px in enumerate(x_peers)
        ]

    def back_core(b):
        for copy in fifth[b]:
            copy.wait_recv()
        sixth[b] = send(qg.at[b, c], qg.at[b, c], s6_s.at[b], s6_r.at[b], (x, y, z, 1 - c))

    local_t(0)
    send_core(0)
    local_t(1)
    send_x(0)
    send_core(1)
    local_t(2)
    send_x(1)
    send_core(2)
    send_x(2)
    gram = lax.dot_general(
        left, left_t, (((1,), (0,)), ((), ())), precision=HIGHEST, preferred_element_type=F32
    )
    packed = jnp.zeros((RANK, 128), F32)
    for b in range(BUCKETS):
        packed = jnp.where(lane // RANK == b, gram[b * RANK : (b + 1) * RANK, :], packed)
    done = jnp.zeros((RANK, 128), F32)
    packed, done = eliminate(packed, done, lane, 0, 8)
    packed, done = eliminate(packed, done, lane, 8, 16)
    for b in range(BUCKETS):
        send_z(b)
    packed, done = eliminate(packed, done, lane, 16, 24)
    packed, done = eliminate(packed, done, lane, 24, 32)
    row = lax.broadcasted_iota(jnp.int32, (RANK, 128), 0)
    inverse = jnp.where(lane % RANK <= row, done, 0.0)
    blocks = [jnp.where(lane // RANK == b, inverse, 0.0) for b in range(BUCKETS)]
    blocks.append(jnp.zeros((RANK, 128), F32))
    factor = jnp.concatenate(blocks, axis=0)
    for b in range(BUCKETS):
        back_z(b)
    basis_t = lax.dot_general(
        left_t[:ROWS], factor, (((1,), (1,)), ((), ())), precision=HIGHEST, preferred_element_type=F32
    )
    weight_t = lax.dot_general(
        basis_t, factor, (((1,), (0,)), ((), ())), precision=HIGHEST, preferred_element_type=F32
    )
    both = jnp.concatenate([weight_t, inverse], axis=0)
    for b in range(BUCKETS):
        high, low = split(both[:, b * RANK : (b + 1) * RANK])
        w_ref[b] = jnp.concatenate([high, low, high, jnp.zeros_like(high)], axis=1)
    for b in range(BUCKETS):
        back_x(b)
    for copy in sends[: -BUCKETS * len(XS)]:
        copy.wait_send()
    del sends[: -BUCKETS * len(XS)]
    for b in range(BUCKETS):
        back_core(b)
    half = width // 2
    for b in range(BUCKETS):
        sixth[b].wait_recv()
        for h in range(2):
            cols = slice(h * half, (h + 1) * half)
            high, low = split(jnp.concatenate([qg[b, h, t] for t in range(4)], axis=0))
            stacked = jnp.concatenate([high, high, low, jnp.zeros_like(high)], axis=0)
            both = dot(w_ref[b], stacked)
            q_ref[b, :, cols] = both[ROWS:]
            err_ref[0, b, :, cols] = c_ref[b, :, cols] - both[:ROWS]
    for copy in sends:
        copy.wait_send()


def per_device(gradient, error_memory, right_factor_initial):
    width = right_factor_initial.shape[2]
    corrected = gradient[0].astype(F32) + error_memory[0]
    half = width // 2
    dma = pltpu.SemaphoreType.DMA
    vmem = pltpu.VMEM
    whole = pl.BlockSpec(memory_space=pltpu.VMEM)
    b3 = BUCKETS
    n_xy, n_x, n_z = len(XY), NX - 1, NZ - 1
    return pl.pallas_call(
        reduce_kernel,
        out_shape=(
            jax.ShapeDtypeStruct((b3, RANK, width), F32),
            jax.ShapeDtypeStruct((1, b3, ROWS, width), F32),
        ),
        in_specs=[whole, whole],
        out_specs=(whole, whole),
        scratch_shapes=[
            vmem((b3, ROWS, width), BF16),
            vmem((b3, ROWS, width), BF16),
            vmem((256, width), BF16),
            vmem((b3, ROWS + RANK, 128), BF16),
            vmem((GROUP, PIECE, 128), F32),
            vmem((n_xy, PIECE, 128), F32),
            vmem((PIECE, 128), F32),
            vmem((PIECE, 128), F32),
            vmem((NZ, PIECE, 128), F32),
            vmem((GROUP, PIECE, 128), F32),
            vmem((256, 128), F32),
            vmem((b3, 2, RANK, half), F32),
            vmem((b3, RANK, half), F32),
            vmem((b3, 4, 8, half), F32),
            vmem((b3, n_x, 8, half), F32),
            vmem((b3, NZ, 8, 128), F32),
            vmem((b3, n_z, 8, 128), F32),
            vmem((b3, NZ, 8, 128), F32),
            vmem((b3, 2, 4, 8, half), F32),
            dma((n_xy,)), dma((n_xy,)),
            dma, dma,
            dma((n_z,)), dma((n_z,)),
            dma((n_xy,)), dma((n_xy,)),
            dma((b3,)), dma((b3,)),
            dma((b3, n_x)), dma((b3, n_x)),
            dma((b3, n_z)), dma((b3, n_z)),
            dma((b3, n_z)), dma((b3, n_z)),
            dma((b3, n_x)), dma((b3, n_x)),
            dma((b3,)), dma((b3,)),
        ],
        compiler_params=pltpu.CompilerParams(
            collective_id=0, has_side_effects=True, vmem_limit_bytes=32 << 20
        ),
        name="reduce_kernel",
    )(corrected, right_factor_initial)


def solution(mesh):
    placed = (P("dp", None, None, "mp"), P("dp", None, None, "mp"), P(None, None, "mp"))
    return jax.shard_map(
        per_device,
        mesh=mesh,
        in_specs=placed,
        out_specs=(P(None, None, "mp"), P("dp", None, None, "mp")),
        check_vma=False,
    )
```

```python
import functools

import jax
import jax.numpy as jnp
from jax import lax
from jax.experimental import pallas as pl
from jax.experimental.pallas import tpu as pltpu
from jax.sharding import PartitionSpec as P

MESH = pl.DeviceIdType.MESH
NX, NY, NZ = 4, 4, 8
BUCKETS, RANK, ROWS = 3, 32, 192
GROUP = NX * NY
PIECE = ROWS // GROUP
PARTS = 9
PART = BUCKETS * ROWS // PARTS
HOPS = [0, 1, 2, 1]
XY = sorted(
    ((i, j) for i in range(NX) for j in range(NY) if i or j), key=lambda p: -HOPS[p[0]] - HOPS[p[1]]
)
XS = [2, 1, 3]
ZS = [4, 3, 5, 2, 6, 1, 7]
F32, BF16 = jnp.float32, jnp.bfloat16
HIGHEST = lax.Precision.HIGHEST


def place():
    dp = lax.axis_index("dp")
    return dp // (2 * NZ), lax.axis_index("mp"), (dp // 2) % NZ, dp % 2


def device(x, y, z, c):
    return ((x * NZ + z) * 2 + c, y)


def split(value):
    high = value.astype(BF16)
    return high, (value - high.astype(F32)).astype(BF16)


def dot(a, b, dims=((1,), (0,))):
    return lax.dot_general(a, b, (dims, ((), ())), preferred_element_type=F32)


def eliminate(z, done, lane, start, stop):
    column = lane % RANK
    row = lax.broadcasted_iota(jnp.int32, (RANK, 128), 0)
    group = lane - column
    cols = [jnp.take_along_axis(z, group + k, axis=1) for k in range(start, stop)]
    for t in range(stop - start):
        k = start + t
        scale = lax.rsqrt(cols[t][k : k + 1, :])
        below = jnp.where(row > k, cols[t] * scale, 0.0)
        pivot = jnp.where(column[k : k + 1] == k, scale, z[k : k + 1, :] * scale)
        done = jnp.where(row == k, pivot, done)
        z = jnp.where(column == k, 0.0, z) - below * pivot
        for u in range(t + 1, stop - start):
            cols[u] = cols[u] - below * (cols[u][k : k + 1, :] * scale)
    return z, done


def reduce_kernel(g_hbm, e_hbm, r_hbm, *refs):
    q_refs, err_refs, refs = refs[:BUCKETS], refs[BUCKETS : BUCKETS + PARTS], refs[BUCKETS + PARTS :]
    (
        g_ref, c_ref, r_ref, ch_ref, cl_ref, rr_ref, w_ref,
        ps, pr, pcs, pcr, zp, pg, pf,
        qs, qc, xs, xr, zs, zr, zg, qg,
        pa_s, pa_r, pc_s, pc_r, pz_s, pz_r, pg_s, pg_r,
        s1_s, s1_r, s2_s, s2_r, s3_s, s3_r, s4_s, s4_r, s5_s, s5_r, s6_s, s6_r,
        in_sem,
    ) = refs
    x, y, z, c = place()
    xy_peers = [((x + i) % NX, (y + j) % NY) for i, j in XY]
    x_peers = [(x + i) % NX for i in XS]
    z_peers = [(z + i) % NZ for i in ZS]
    mine = x * NY + y

    loads = [pltpu.make_async_copy(r_hbm, r_ref, in_sem.at[0])]
    for b in range(BUCKETS):
        loads.append(pltpu.make_async_copy(g_hbm.at[0, b], g_ref.at[b], in_sem.at[1 + 2 * b]))
        loads.append(pltpu.make_async_copy(e_hbm.at[0, b], c_ref.at[b], in_sem.at[2 + 2 * b]))
    for load in loads:
        load.start()

    barrier = pltpu.get_barrier_semaphore()
    for px, py in xy_peers:
        pl.semaphore_signal(barrier, inc=1, device_id=device(px, py, z, c), device_id_type=MESH)
    for pz in z_peers:
        pl.semaphore_signal(barrier, inc=1, device_id=device(x, y, pz, c), device_id_type=MESH)
    pl.semaphore_signal(barrier, inc=1, device_id=device(x, y, z, 1 - c), device_id_type=MESH)

    sends = []

    def send(src, dst, send_sem, recv_sem, where):
        copy = pltpu.make_async_remote_copy(
            src_ref=src, dst_ref=dst, send_sem=send_sem, recv_sem=recv_sem,
            device_id=device(*where), device_id_type=MESH,
        )
        copy.start()
        sends.append(copy)
        return copy

    width = r_ref.shape[2]
    loads[0].wait()
    rr_ref[...] = jnp.zeros_like(rr_ref)
    for b in range(BUCKETS):
        high, low = split(r_ref[b])
        rr_ref[b * RANK : (b + 1) * RANK, :] = high
        rr_ref[128 + b * RANK : 128 + (b + 1) * RANK, :] = low

    lane = lax.broadcasted_iota(jnp.int32, (RANK, 128), 1)
    lane_rows = lax.broadcasted_iota(jnp.int32, (ROWS, 128), 1)
    step = 256
    total = jnp.zeros((ROWS, 128), F32)
    for b in range(BUCKETS):
        loads[1 + 2 * b].wait()
        loads[2 + 2 * b].wait()
        both = jnp.zeros((ROWS, 256), F32)
        rest = jnp.zeros((ROWS, 128), F32)
        for start in range(0, width, step):
            cols = slice(start, start + step)
            value = g_ref[b, :, cols].astype(F32) + c_ref[b, :, cols]
            c_ref[b, :, cols] = value
            high, low = split(value)
            ch_ref[b, :, cols] = high
            cl_ref[b, :, cols] = low
            both = both + dot(high, rr_ref[:, cols], ((1,), (1,)))
            rest = rest + dot(low, rr_ref[:128, cols], ((1,), (1,)))
        part = both[:, :128] + both[:, 128:] + rest
        total = jnp.where(lane_rows // RANK == b, part, total)
    total = total * (1.0 / 64)
    for i in range(GROUP):
        ps[i] = total[i * PIECE : (i + 1) * PIECE, :]

    pl.semaphore_wait(barrier, len(XY) + NZ)

    copies = [
        send(ps.at[px * NY + py], pr.at[i], pa_s.at[i], pa_r.at[i], (px, py, z, c))
        for i, (px, py) in enumerate(xy_peers)
    ]
    piece = ps[mine]
    for i, copy in enumerate(copies):
        copy.wait_recv()
        piece = piece + pr[i]
    pcs[...] = piece
    copy = send(pcs, pcr, pc_s, pc_r, (x, y, z, 1 - c))
    copy.wait_recv()
    piece = piece + pcr[...]
    zp[z] = piece
    copies = [
        send(zp.at[z], zp.at[z], pz_s.at[i], pz_r.at[i], (x, y, at, c)) for i, at in enumerate(z_peers)
    ]
    for copy in copies:
        copy.wait_recv()
    piece = zp[0]
    for i in range(1, NZ):
        piece = piece + zp[i]
    pg[mine] = piece
    copies = [
        send(pg.at[mine], pg.at[mine], pg_s.at[i], pg_r.at[i], (px, py, z, c))
        for i, (px, py) in enumerate(xy_peers)
    ]
    for copy in copies:
        copy.wait_recv()
    for i in range(GROUP):
        pf[i * PIECE : (i + 1) * PIECE, :] = pg[i]
    pf[ROWS:, :] = jnp.zeros((256 - ROWS, 128), F32)

    left_t = pf[...]
    left = left_t.T
    left_high, left_low = split(left[:, :ROWS])

    def local_t(b):
        rows = slice(b * RANK, (b + 1) * RANK)
        stacked = jnp.concatenate([left_high[rows], left_low[rows]], axis=0)
        half = width // 2
        for start in range(0, width, 256):
            stop = start + 256
            one = dot(stacked, ch_ref[b, :, start:stop])
            value = one[:RANK] + one[RANK:] + dot(left_high[rows], cl_ref[b, :, start:stop])
            if stop <= half:
                qs[b, 0, :, start:stop] = value
            elif start >= half:
                qs[b, 1, :, start - half : stop - half] = value
            else:
                qs[b, 0, :, start:half] = value[:, : half - start]
                qs[b, 1, :, : stop - half] = value[:, half - start :]

    first, second, third, fourth, fifth, sixth = ({} for _ in range(6))
    tiles = width // 2 // 128

    def send_core(b):
        first[b] = send(qs.at[b, 1 - c], qc.at[b], s1_s.at[b], s1_r.at[b], (x, y, z, 1 - c))

    def send_x(b):
        first[b].wait_recv()
        for t in range(4):
            xs[b, t] = qs[b, c, 8 * t : 8 * t + 8, :] + qc[b, 8 * t : 8 * t + 8, :]
        second[b] = [
            send(xs.at[b, px], xr.at[b, i], s2_s.at[b, i], s2_r.at[b, i], (px, y, z, c))
            for i, px in enumerate(x_peers)
        ]

    def send_z(b):
        value = xs[b, x]
        for i, copy in enumerate(second[b]):
            copy.wait_recv()
            value = value + xr[b, i]
        for t in range(tiles):
            zs[b, t] = value[:, t * 128 : (t + 1) * 128]
        zs[b, tiles] = jnp.zeros((8, 128), F32)
        third[b] = [
            send(zs.at[b, pz], zr.at[b, i], s3_s.at[b, i], s3_r.at[b, i], (x, y, pz, c))
            for i, pz in enumerate(z_peers)
        ]

    def back_z(b):
        value = zs[b, z]
        for i, copy in enumerate(third[b]):
            copy.wait_recv()
            value = value + zr[b, i]
        zg[b, z] = value * (1.0 / 64)
        fourth[b] = [
            send(zg.at[b, z], zg.at[b, z], s4_s.at[b, i], s4_r.at[b, i], (x, y, pz, c))
            for i, pz in enumerate(z_peers)
        ]

    def back_x(b):
        for copy in fourth[b]:
            copy.wait_recv()
        for t in range(tiles):
            qg[b, c, x, :, t * 128 : (t + 1) * 128] = zg[b, t]
        fifth[b] = [
            send(qg.at[b, c, x], qg.at[b, c, x], s5_s.at[b, i], s5_r.at[b, i], (px, y, z, c))
            for i, px in enumerate(x_peers)
        ]

    def back_core(b):
        for copy in fifth[b]:
            copy.wait_recv()
        sixth[b] = send(qg.at[b, c], qg.at[b, c], s6_s.at[b], s6_r.at[b], (x, y, z, 1 - c))

    for b in range(BUCKETS):
        local_t(b)
        send_core(b)
    for b in range(BUCKETS):
        send_x(b)
    gram = lax.dot_general(
        left, left_t, (((1,), (0,)), ((), ())), precision=HIGHEST, preferred_element_type=F32
    )
    packed = jnp.zeros((RANK, 128), F32)
    for b in range(BUCKETS):
        packed = jnp.where(lane // RANK == b, gram[b * RANK : (b + 1) * RANK, :], packed)
    done = jnp.zeros((RANK, 128), F32)
    packed, done = eliminate(packed, done, lane, 0, 8)
    packed, done = eliminate(packed, done, lane, 8, 16)
    for b in range(BUCKETS):
        send_z(b)
    packed, done = eliminate(packed, done, lane, 16, 24)
    packed, done = eliminate(packed, done, lane, 24, 32)
    row = lax.broadcasted_iota(jnp.int32, (RANK, 128), 0)
    inverse = jnp.where(lane % RANK <= row, done, 0.0)
    blocks = [jnp.where(lane // RANK == b, inverse, 0.0) for b in range(BUCKETS)]
    blocks.append(jnp.zeros((RANK, 128), F32))
    factor = jnp.concatenate(blocks, axis=0)
    for b in range(BUCKETS):
        back_z(b)
    basis_t = lax.dot_general(
        left_t[:ROWS], factor, (((1,), (1,)), ((), ())), precision=HIGHEST, preferred_element_type=F32
    )
    weight_t = lax.dot_general(
        basis_t, factor, (((1,), (0,)), ((), ())), precision=HIGHEST, preferred_element_type=F32
    )
    both = jnp.concatenate([weight_t, inverse], axis=0)
    for b in range(BUCKETS):
        high, low = split(both[:, b * RANK : (b + 1) * RANK])
        w_ref[b] = jnp.concatenate([high, low, high, jnp.zeros_like(high)], axis=1)
    for b in range(BUCKETS):
        back_x(b)
    for copy in sends[: -BUCKETS * len(XS)]:
        copy.wait_send()
    del sends[: -BUCKETS * len(XS)]
    for b in range(BUCKETS):
        back_core(b)
    half = width // 2
    for b in range(BUCKETS):
        sixth[b].wait_recv()
        for h in range(2):
            cols = slice(h * half, (h + 1) * half)
            high, low = split(jnp.concatenate([qg[b, h, t] for t in range(4)], axis=0))
            stacked = jnp.concatenate([high, high, low, jnp.zeros_like(high)], axis=0)
            both = dot(w_ref[b], stacked)
            q_refs[b][:, cols] = both[ROWS:]
            for i in range(PARTS // BUCKETS):
                rows = slice(i * PART, (i + 1) * PART)
                err_refs[b * (PARTS // BUCKETS) + i][:, cols] = c_ref[b, rows, cols] - both[rows]
    for copy in sends:
        copy.wait_send()


def store_kernel(*refs):
    parts, (q_out, err_out, sem) = refs[:-3], refs[-3:]
    copies = []
    for i in range(PARTS):
        b, row = divmod(i * PART, ROWS)
        rows = pl.ds(row, PART)
        copies.append(
            pltpu.make_async_copy(parts[BUCKETS + i], err_out.at[0, b, rows], sem.at[BUCKETS + i])
        )
    for b in range(BUCKETS):
        copies.append(pltpu.make_async_copy(parts[b], q_out.at[b], sem.at[b]))
    for copy in copies:
        copy.start()
    for copy in copies:
        copy.wait()


def per_device(gradient, error_memory, right_factor_initial):
    width = right_factor_initial.shape[2]
    half = width // 2
    dma = pltpu.SemaphoreType.DMA
    vmem = pltpu.VMEM
    whole = pl.BlockSpec(memory_space=pltpu.VMEM)
    hbm = pl.BlockSpec(memory_space=pl.ANY)
    b3 = BUCKETS
    n_xy, n_x, n_z = len(XY), NX - 1, NZ - 1
    made = pl.pallas_call(
        reduce_kernel,
        out_shape=(jax.ShapeDtypeStruct((RANK, width), F32),) * b3
        + (jax.ShapeDtypeStruct((PART, width), F32),) * PARTS,
        in_specs=[hbm] * 3,
        out_specs=(whole,) * (b3 + PARTS),
        scratch_shapes=[
            vmem((b3, ROWS, width), BF16),
            vmem((b3, ROWS, width), F32),
            vmem((b3, RANK, width), F32),
            vmem((b3, ROWS, width), BF16),
            vmem((b3, ROWS, width), BF16),
            vmem((256, width), BF16),
            vmem((b3, ROWS + RANK, 128), BF16),
            vmem((GROUP, PIECE, 128), F32),
            vmem((n_xy, PIECE, 128), F32),
            vmem((PIECE, 128), F32),
            vmem((PIECE, 128), F32),
            vmem((NZ, PIECE, 128), F32),
            vmem((GROUP, PIECE, 128), F32),
            vmem((256, 128), F32),
            vmem((b3, 2, RANK, half), F32),
            vmem((b3, RANK, half), F32),
            vmem((b3, 4, 8, half), F32),
            vmem((b3, n_x, 8, half), F32),
            vmem((b3, NZ, 8, 128), F32),
            vmem((b3, n_z, 8, 128), F32),
            vmem((b3, NZ, 8, 128), F32),
            vmem((b3, 2, 4, 8, half), F32),
            dma((n_xy,)), dma((n_xy,)),
            dma, dma,
            dma((n_z,)), dma((n_z,)),
            dma((n_xy,)), dma((n_xy,)),
            dma((b3,)), dma((b3,)),
            dma((b3, n_x)), dma((b3, n_x)),
            dma((b3, n_z)), dma((b3, n_z)),
            dma((b3, n_z)), dma((b3, n_z)),
            dma((b3, n_x)), dma((b3, n_x)),
            dma((b3,)), dma((b3,)),
            dma((1 + 2 * b3,)),
        ],
        compiler_params=pltpu.CompilerParams(
            collective_id=0, has_side_effects=True, vmem_limit_bytes=49 << 20
        ),
        name="reduce_kernel",
    )(gradient, error_memory, right_factor_initial)
    return pl.pallas_call(
        store_kernel,
        out_shape=(
            jax.ShapeDtypeStruct((b3, RANK, width), F32),
            jax.ShapeDtypeStruct((1, b3, ROWS, width), F32),
        ),
        in_specs=[hbm] * (b3 + PARTS),
        out_specs=(hbm, hbm),
        scratch_shapes=[dma((b3 + PARTS,))],
        compiler_params=pltpu.CompilerParams(vmem_limit_bytes=1 << 20),
        name="store_kernel",
    )(*made)


def solution(mesh):
    placed = (P("dp", None, None, "mp"), P("dp", None, None, "mp"), P(None, None, "mp"))
    return jax.shard_map(
        per_device,
        mesh=mesh,
        in_specs=placed,
        out_specs=(P(None, None, "mp"), P("dp", None, None, "mp")),
        check_vma=False,
    )
```

```python
import functools

import jax
import jax.numpy as jnp
from jax import lax
from jax.experimental import pallas as pl
from jax.experimental.pallas import tpu as pltpu
from jax.sharding import PartitionSpec as P

MESH = pl.DeviceIdType.MESH
NX, NY, NZ = 4, 4, 8
BUCKETS, RANK, ROWS = 3, 32, 192
GROUP = NX * NY
PIECE = ROWS // GROUP
PARTS = 9
PART = BUCKETS * ROWS // PARTS
HOPS = [0, 1, 2, 1]
XY = sorted(
    ((i, j) for i in range(NX) for j in range(NY) if i or j), key=lambda p: -HOPS[p[0]] - HOPS[p[1]]
)
XS = [2, 1, 3]
ZS = [4, 3, 5, 2, 6, 1, 7]
F32, BF16 = jnp.float32, jnp.bfloat16
HIGHEST = lax.Precision.HIGHEST


def place():
    dp = lax.axis_index("dp")
    return dp // (2 * NZ), lax.axis_index("mp"), (dp // 2) % NZ, dp % 2


def device(x, y, z, c):
    return ((x * NZ + z) * 2 + c, y)


def split(value):
    high = value.astype(BF16)
    return high, (value - high.astype(F32)).astype(BF16)


def dot(a, b, dims=((1,), (0,))):
    return lax.dot_general(a, b, (dims, ((), ())), preferred_element_type=F32)


def eliminate(z, done, lane, start, stop):
    column = lane % RANK
    row = lax.broadcasted_iota(jnp.int32, (RANK, 128), 0)
    group = lane - column
    cols = [jnp.take_along_axis(z, group + k, axis=1) for k in range(start, stop)]
    for t in range(stop - start):
        k = start + t
        scale = lax.rsqrt(cols[t][k : k + 1, :])
        below = jnp.where(row > k, cols[t] * scale, 0.0)
        pivot = jnp.where(column[k : k + 1] == k, scale, z[k : k + 1, :] * scale)
        done = jnp.where(row == k, pivot, done)
        z = jnp.where(column == k, 0.0, z) - below * pivot
        for u in range(t + 1, stop - start):
            cols[u] = cols[u] - below * (cols[u][k : k + 1, :] * scale)
    return z, done


def reduce_kernel(g_hbm, e_hbm, r_hbm, *refs):
    q_refs, err_refs, refs = refs[:BUCKETS], refs[BUCKETS : BUCKETS + PARTS], refs[BUCKETS + PARTS :]
    (
        g_ref, c_ref, r_ref, ch_ref, cl_ref, rr_ref, w_ref,
        ps, pr, pcs, pcr, zp, pg, pf,
        qs, qc, xs, xr, zs, zr, zg, qg,
        pa_s, pa_r, pc_s, pc_r, pz_s, pz_r, pg_s, pg_r,
        s1_s, s1_r, s2_s, s2_r, s3_s, s3_r, s4_s, s4_r, s5_s, s5_r, s6_s, s6_r,
        in_sem,
    ) = refs
    x, y, z, c = place()
    xy_peers = [((x + i) % NX, (y + j) % NY) for i, j in XY]
    x_peers = [(x + i) % NX for i in XS]
    z_peers = [(z + i) % NZ for i in ZS]
    mine = x * NY + y

    loads = [pltpu.make_async_copy(r_hbm, r_ref, in_sem.at[0])]
    for b in range(BUCKETS):
        loads.append(pltpu.make_async_copy(g_hbm.at[0, b], g_ref.at[b], in_sem.at[1 + 2 * b]))
        loads.append(pltpu.make_async_copy(e_hbm.at[0, b], c_ref.at[b], in_sem.at[2 + 2 * b]))
    for load in loads:
        load.start()

    barrier = pltpu.get_barrier_semaphore()
    for px, py in xy_peers:
        pl.semaphore_signal(barrier, inc=1, device_id=device(px, py, z, c), device_id_type=MESH)
    for pz in z_peers:
        pl.semaphore_signal(barrier, inc=1, device_id=device(x, y, pz, c), device_id_type=MESH)
    pl.semaphore_signal(barrier, inc=1, device_id=device(x, y, z, 1 - c), device_id_type=MESH)

    def send(src, dst, send_sem, recv_sem, where):
        pltpu.make_async_remote_copy(
            src_ref=src, dst_ref=dst, send_sem=send_sem, recv_sem=recv_sem,
            device_id=device(*where), device_id_type=MESH,
        ).start()

    def wait(like, sem):
        pltpu.make_async_copy(like, like, sem).wait()

    width = r_ref.shape[2]
    loads[0].wait()
    rr_ref[...] = jnp.zeros_like(rr_ref)
    for b in range(BUCKETS):
        high, low = split(r_ref[b])
        rr_ref[b * RANK : (b + 1) * RANK, :] = high
        rr_ref[128 + b * RANK : 128 + (b + 1) * RANK, :] = low

    lane = lax.broadcasted_iota(jnp.int32, (RANK, 128), 1)
    lane_rows = lax.broadcasted_iota(jnp.int32, (ROWS, 128), 1)
    step = 256
    total = jnp.zeros((ROWS, 128), F32)
    for b in range(BUCKETS):
        loads[1 + 2 * b].wait()
        loads[2 + 2 * b].wait()
        both = jnp.zeros((ROWS, 256), F32)
        rest = jnp.zeros((ROWS, 128), F32)
        for start in range(0, width, step):
            cols = slice(start, start + step)
            value = g_ref[b, :, cols].astype(F32) + c_ref[b, :, cols]
            c_ref[b, :, cols] = value
            high, low = split(value)
            ch_ref[b, :, cols] = high
            cl_ref[b, :, cols] = low
            both = both + dot(high, rr_ref[:, cols], ((1,), (1,)))
            rest = rest + dot(low, rr_ref[:128, cols], ((1,), (1,)))
        part = both[:, :128] + both[:, 128:] + rest
        total = jnp.where(lane_rows // RANK == b, part, total)
    total = total * (1.0 / 64)
    for i in range(GROUP):
        ps[i] = total[i * PIECE : (i + 1) * PIECE, :]

    pl.semaphore_wait(barrier, len(XY) + NZ)

    for i, (px, py) in enumerate(xy_peers):
        send(ps.at[px * NY + py], pr.at[i], pa_s, pa_r, (px, py, z, c))
    piece = ps[mine]
    wait(pr, pa_r)
    for i in range(len(XY)):
        piece = piece + pr[i]
    pcs[...] = piece
    send(pcs, pcr, pc_s, pc_r, (x, y, z, 1 - c))
    wait(pcr, pc_r)
    zp[z] = piece + pcr[...]
    for pz in z_peers:
        send(zp.at[z], zp.at[z], pz_s, pz_r, (x, y, pz, c))
    wait(zp.at[: NZ - 1], pz_r)
    piece = zp[0]
    for i in range(1, NZ):
        piece = piece + zp[i]
    pg[mine] = piece
    for px, py in xy_peers:
        send(pg.at[mine], pg.at[mine], pg_s, pg_r, (px, py, z, c))
    wait(pg.at[: GROUP - 1], pg_r)
    for i in range(GROUP):
        pf[i * PIECE : (i + 1) * PIECE, :] = pg[i]
    pf[ROWS:, :] = jnp.zeros((256 - ROWS, 128), F32)

    left_t = pf[...]
    left = left_t.T
    left_high, left_low = split(left[:, :ROWS])

    def local_t(b):
        rows = slice(b * RANK, (b + 1) * RANK)
        stacked = jnp.concatenate([left_high[rows], left_low[rows]], axis=0)
        half = width // 2
        for start in range(0, width, 256):
            stop = start + 256
            one = dot(stacked, ch_ref[b, :, start:stop])
            value = one[:RANK] + one[RANK:] + dot(left_high[rows], cl_ref[b, :, start:stop])
            if stop <= half:
                qs[b, 0, :, start:stop] = value
            elif start >= half:
                qs[b, 1, :, start - half : stop - half] = value
            else:
                qs[b, 0, :, start:half] = value[:, : half - start]
                qs[b, 1, :, : stop - half] = value[:, half - start :]

    tiles = width // 2 // 128

    def send_core(b):
        send(qs.at[b, 1 - c], qc.at[b], s1_s.at[b], s1_r.at[b], (x, y, z, 1 - c))

    def send_x(b):
        wait(qc.at[b], s1_r.at[b])
        for t in range(4):
            xs[b, t] = qs[b, c, 8 * t : 8 * t + 8, :] + qc[b, 8 * t : 8 * t + 8, :]
        for i, px in enumerate(x_peers):
            send(xs.at[b, px], xr.at[b, i], s2_s.at[b], s2_r.at[b], (px, y, z, c))

    def send_z(b):
        value = xs[b, x]
        wait(xr.at[b], s2_r.at[b])
        for i in range(NX - 1):
            value = value + xr[b, i]
        for t in range(tiles):
            zs[b, t] = value[:, t * 128 : (t + 1) * 128]
        zs[b, tiles] = jnp.zeros((8, 128), F32)
        for i, pz in enumerate(z_peers):
            send(zs.at[b, pz], zr.at[b, i], s3_s.at[b], s3_r.at[b], (x, y, pz, c))

    def back_z(b):
        value = zs[b, z]
        wait(zr.at[b], s3_r.at[b])
        for i in range(NZ - 1):
            value = value + zr[b, i]
        zg[b, z] = value * (1.0 / 64)
        for pz in z_peers:
            send(zg.at[b, z], zg.at[b, z], s4_s.at[b], s4_r.at[b], (x, y, pz, c))

    def back_x(b):
        wait(zg.at[b, : NZ - 1], s4_r.at[b])
        for t in range(tiles):
            qg[b, c, x, :, t * 128 : (t + 1) * 128] = zg[b, t]
        for px in x_peers:
            send(qg.at[b, c, x], qg.at[b, c, x], s5_s.at[b], s5_r.at[b], (px, y, z, c))

    def back_core(b):
        wait(qg.at[b, c, : NX - 1], s5_r.at[b])
        send(qg.at[b, c], qg.at[b, c], s6_s.at[b], s6_r.at[b], (x, y, z, 1 - c))

    for b in range(BUCKETS):
        local_t(b)
        send_core(b)
    for b in range(BUCKETS):
        send_x(b)
    gram = lax.dot_general(
        left, left_t, (((1,), (0,)), ((), ())), precision=HIGHEST, preferred_element_type=F32
    )
    packed = jnp.zeros((RANK, 128), F32)
    for b in range(BUCKETS):
        packed = jnp.where(lane // RANK == b, gram[b * RANK : (b + 1) * RANK, :], packed)
    done = jnp.zeros((RANK, 128), F32)
    packed, done = eliminate(packed, done, lane, 0, 8)
    packed, done = eliminate(packed, done, lane, 8, 16)
    for b in range(BUCKETS):
        send_z(b)
    packed, done = eliminate(packed, done, lane, 16, 24)
    packed, done = eliminate(packed, done, lane, 24, 32)
    row = lax.broadcasted_iota(jnp.int32, (RANK, 128), 0)
    inverse = jnp.where(lane % RANK <= row, done, 0.0)
    blocks = [jnp.where(lane // RANK == b, inverse, 0.0) for b in range(BUCKETS)]
    blocks.append(jnp.zeros((RANK, 128), F32))
    factor = jnp.concatenate(blocks, axis=0)
    for b in range(BUCKETS):
        back_z(b)
    basis_t = lax.dot_general(
        left_t[:ROWS], factor, (((1,), (1,)), ((), ())), precision=HIGHEST, preferred_element_type=F32
    )
    weight_t = lax.dot_general(
        basis_t, factor, (((1,), (0,)), ((), ())), precision=HIGHEST, preferred_element_type=F32
    )
    both = jnp.concatenate([weight_t, inverse], axis=0)
    for b in range(BUCKETS):
        high, low = split(both[:, b * RANK : (b + 1) * RANK])
        w_ref[b] = jnp.concatenate([high, low, high, jnp.zeros_like(high)], axis=1)
    for b in range(BUCKETS):
        back_x(b)
    wait(pr, pa_s)
    wait(pcs, pc_s)
    wait(zp.at[: NZ - 1], pz_s)
    wait(pg.at[: GROUP - 1], pg_s)
    for b in range(BUCKETS):
        wait(qc.at[b], s1_s.at[b])
        wait(xr.at[b], s2_s.at[b])
        wait(zr.at[b], s3_s.at[b])
        wait(zg.at[b, : NZ - 1], s4_s.at[b])
    for b in range(BUCKETS):
        back_core(b)
    half = width // 2
    for b in range(BUCKETS):
        wait(qg.at[b, 1 - c], s6_r.at[b])
        for h in range(2):
            cols = slice(h * half, (h + 1) * half)
            high, low = split(jnp.concatenate([qg[b, h, t] for t in range(4)], axis=0))
            stacked = jnp.concatenate([high, high, low, jnp.zeros_like(high)], axis=0)
            both = dot(w_ref[b], stacked)
            q_refs[b][:, cols] = both[ROWS:]
            for i in range(PARTS // BUCKETS):
                rows = slice(i * PART, (i + 1) * PART)
                err_refs[b * (PARTS // BUCKETS) + i][:, cols] = c_ref[b, rows, cols] - both[rows]
    for b in range(BUCKETS):
        wait(qg.at[b, c, : NX - 1], s5_s.at[b])
        wait(qg.at[b, c], s6_s.at[b])


def store_kernel(*refs):
    parts, (q_out, err_out, sem) = refs[:-3], refs[-3:]
    copies = []
    for i in range(PARTS):
        b, row = divmod(i * PART, ROWS)
        rows = pl.ds(row, PART)
        copies.append(
            pltpu.make_async_copy(parts[BUCKETS + i], err_out.at[0, b, rows], sem.at[BUCKETS + i])
        )
    for b in range(BUCKETS):
        copies.append(pltpu.make_async_copy(parts[b], q_out.at[b], sem.at[b]))
    for copy in copies:
        copy.start()
    for copy in copies:
        copy.wait()


def per_device(gradient, error_memory, right_factor_initial):
    width = right_factor_initial.shape[2]
    half = width // 2
    dma = pltpu.SemaphoreType.DMA
    vmem = pltpu.VMEM
    whole = pl.BlockSpec(memory_space=pltpu.VMEM)
    hbm = pl.BlockSpec(memory_space=pl.ANY)
    b3 = BUCKETS
    n_xy, n_x, n_z = len(XY), NX - 1, NZ - 1
    made = pl.pallas_call(
        reduce_kernel,
        out_shape=(jax.ShapeDtypeStruct((RANK, width), F32),) * b3
        + (jax.ShapeDtypeStruct((PART, width), F32),) * PARTS,
        in_specs=[hbm] * 3,
        out_specs=(whole,) * (b3 + PARTS),
        scratch_shapes=[
            vmem((b3, ROWS, width), BF16),
            vmem((b3, ROWS, width), F32),
            vmem((b3, RANK, width), F32),
            vmem((b3, ROWS, width), BF16),
            vmem((b3, ROWS, width), BF16),
            vmem((256, width), BF16),
            vmem((b3, ROWS + RANK, 128), BF16),
            vmem((GROUP, PIECE, 128), F32),
            vmem((n_xy, PIECE, 128), F32),
            vmem((PIECE, 128), F32),
            vmem((PIECE, 128), F32),
            vmem((NZ, PIECE, 128), F32),
            vmem((GROUP, PIECE, 128), F32),
            vmem((256, 128), F32),
            vmem((b3, 2, RANK, half), F32),
            vmem((b3, RANK, half), F32),
            vmem((b3, 4, 8, half), F32),
            vmem((b3, n_x, 8, half), F32),
            vmem((b3, NZ, 8, 128), F32),
            vmem((b3, n_z, 8, 128), F32),
            vmem((b3, NZ, 8, 128), F32),
            vmem((b3, 2, 4, 8, half), F32),
            *([dma] * 8),
            *([dma((b3,))] * 12),
            dma((1 + 2 * b3,)),
        ],
        compiler_params=pltpu.CompilerParams(
            collective_id=0, has_side_effects=True, vmem_limit_bytes=49 << 20
        ),
        name="reduce_kernel",
    )(gradient, error_memory, right_factor_initial)
    return pl.pallas_call(
        store_kernel,
        out_shape=(
            jax.ShapeDtypeStruct((b3, RANK, width), F32),
            jax.ShapeDtypeStruct((1, b3, ROWS, width), F32),
        ),
        in_specs=[hbm] * (b3 + PARTS),
        out_specs=(hbm, hbm),
        scratch_shapes=[dma((b3 + PARTS,))],
        compiler_params=pltpu.CompilerParams(vmem_limit_bytes=1 << 20),
        name="store_kernel",
    )(*made)


def solution(mesh):
    placed = (P("dp", None, None, "mp"), P("dp", None, None, "mp"), P(None, None, "mp"))
    return jax.shard_map(
        per_device,
        mesh=mesh,
        in_specs=placed,
        out_specs=(P(None, None, "mp"), P("dp", None, None, "mp")),
        check_vma=False,
    )
```

```python
import functools

import jax
import jax.numpy as jnp
from jax import lax
from jax.experimental import pallas as pl
from jax.experimental.pallas import tpu as pltpu
from jax.sharding import PartitionSpec as P

MESH = pl.DeviceIdType.MESH
NX, NY, NZ = 4, 4, 8
BUCKETS, RANK, ROWS = 3, 32, 192
GROUP = NX * NY
PIECE = ROWS // GROUP
PARTS = 9
PART = BUCKETS * ROWS // PARTS
HOPS = [0, 1, 2, 1]
XY = sorted(
    ((i, j) for i in range(NX) for j in range(NY) if i or j), key=lambda p: -HOPS[p[0]] - HOPS[p[1]]
)
XS = [2, 1, 3]
ZS = [4, 3, 5, 2, 6, 1, 7]
F32, BF16 = jnp.float32, jnp.bfloat16
HIGHEST = lax.Precision.HIGHEST


def place():
    dp = lax.axis_index("dp")
    return dp // (2 * NZ), lax.axis_index("mp"), (dp // 2) % NZ, dp % 2


def device(x, y, z, c):
    return ((x * NZ + z) * 2 + c, y)


def split(value):
    high = value.astype(BF16)
    return high, (value - high.astype(F32)).astype(BF16)


def dot(a, b, dims=((1,), (0,))):
    return lax.dot_general(a, b, (dims, ((), ())), preferred_element_type=F32)


def eliminate(z, done, lane, start, stop):
    column = lane % RANK
    row = lax.broadcasted_iota(jnp.int32, (RANK, 128), 0)
    group = lane - column
    cols = [jnp.take_along_axis(z, group + k, axis=1) for k in range(start, stop)]
    for t in range(stop - start):
        k = start + t
        scale = lax.rsqrt(cols[t][k : k + 1, :])
        below = jnp.where(row > k, cols[t] * scale, 0.0)
        pivot = jnp.where(column[k : k + 1] == k, scale, z[k : k + 1, :] * scale)
        done = jnp.where(row == k, pivot, done)
        z = jnp.where(column == k, 0.0, z) - below * pivot
        for u in range(t + 1, stop - start):
            cols[u] = cols[u] - below * (cols[u][k : k + 1, :] * scale)
    return z, done


def reduce_kernel(g_hbm, e_hbm, r_hbm, *refs):
    q_refs, err_refs, refs = refs[:BUCKETS], refs[BUCKETS : BUCKETS + PARTS], refs[BUCKETS + PARTS :]
    (
        g_ref, c_ref, r_ref, ch_ref, cl_ref, rr_ref, w_ref,
        ps, pr, pcs, pcr, zp, pg, pf,
        qs, qc, xs, xr, zs, zr, zg, qg,
        pa_s, pa_r, pc_s, pc_r, pz_s, pz_r, pg_s, pg_r,
        s1_s, s1_r, s2_s, s2_r, s3_s, s3_r, s4_s, s4_r, s5_s, s5_r, s6_s, s6_r,
        in_sem, fzs, fzr, fxs, fxr, fxg, fzg,
    ) = refs
    x, y, z, c = place()
    xy_peers = [((x + i) % NX, (y + j) % NY) for i, j in XY]
    x_peers = [(x + i) % NX for i in XS]
    z_peers = [(z + i) % NZ for i in ZS]
    mine = x * NY + y

    loads = [pltpu.make_async_copy(r_hbm, r_ref, in_sem.at[0])]
    for b in range(BUCKETS):
        loads.append(pltpu.make_async_copy(g_hbm.at[0, b], g_ref.at[b], in_sem.at[1 + 2 * b]))
        loads.append(pltpu.make_async_copy(e_hbm.at[0, b], c_ref.at[b], in_sem.at[2 + 2 * b]))
    for load in loads:
        load.start()

    barrier = pltpu.get_barrier_semaphore()
    for px, py in xy_peers:
        pl.semaphore_signal(barrier, inc=1, device_id=device(px, py, z, c), device_id_type=MESH)
    for pz in z_peers:
        pl.semaphore_signal(barrier, inc=1, device_id=device(x, y, pz, c), device_id_type=MESH)
    pl.semaphore_signal(barrier, inc=1, device_id=device(x, y, z, 1 - c), device_id_type=MESH)

    def send(src, dst, send_sem, recv_sem, where):
        pltpu.make_async_remote_copy(
            src_ref=src, dst_ref=dst, send_sem=send_sem, recv_sem=recv_sem,
            device_id=device(*where), device_id_type=MESH,
        ).start()

    def wait(like, sem):
        pltpu.make_async_copy(like, like, sem).wait()

    width = r_ref.shape[2]
    loads[0].wait()
    rr_ref[...] = jnp.zeros_like(rr_ref)
    for b in range(BUCKETS):
        high, low = split(r_ref[b])
        rr_ref[b * RANK : (b + 1) * RANK, :] = high
        rr_ref[128 + b * RANK : 128 + (b + 1) * RANK, :] = low

    lane = lax.broadcasted_iota(jnp.int32, (RANK, 128), 1)
    lane_rows = lax.broadcasted_iota(jnp.int32, (ROWS, 128), 1)
    step = 256
    total = jnp.zeros((ROWS, 128), F32)
    for b in range(BUCKETS):
        loads[1 + 2 * b].wait()
        loads[2 + 2 * b].wait()
        both = jnp.zeros((ROWS, 256), F32)
        rest = jnp.zeros((ROWS, 128), F32)
        for start in range(0, width, step):
            cols = slice(start, start + step)
            value = g_ref[b, :, cols].astype(F32) + c_ref[b, :, cols]
            c_ref[b, :, cols] = value
            high, low = split(value)
            ch_ref[b, :, cols] = high
            cl_ref[b, :, cols] = low
            both = both + dot(high, rr_ref[:, cols], ((1,), (1,)))
            rest = rest + dot(low, rr_ref[:128, cols], ((1,), (1,)))
        part = both[:, :128] + both[:, 128:] + rest
        total = jnp.where(lane_rows // RANK == b, part, total)
    total = total * (1.0 / 64)
    for i in range(GROUP):
        ps[i] = total[i * PIECE : (i + 1) * PIECE, :]

    pl.semaphore_wait(barrier, len(XY) + NZ)

    for i, (px, py) in enumerate(xy_peers):
        send(ps.at[px * NY + py], pr.at[i], pa_s, pa_r, (px, py, z, c))
    piece = ps[mine]
    wait(pr, pa_r)
    for i in range(len(XY)):
        piece = piece + pr[i]
    pcs[...] = piece
    send(pcs, pcr, pc_s, pc_r, (x, y, z, 1 - c))
    wait(pcr, pc_r)
    zp[z] = piece + pcr[...]
    for pz in z_peers:
        send(zp.at[z], zp.at[z], pz_s, pz_r, (x, y, pz, c))
    wait(zp.at[: NZ - 1], pz_r)
    piece = zp[0]
    for i in range(1, NZ):
        piece = piece + zp[i]
    pg[mine] = piece
    for px, py in xy_peers:
        send(pg.at[mine], pg.at[mine], pg_s, pg_r, (px, py, z, c))
    wait(pg.at[: GROUP - 1], pg_r)
    for i in range(GROUP):
        pf[i * PIECE : (i + 1) * PIECE, :] = pg[i]
    pf[ROWS:, :] = jnp.zeros((256 - ROWS, 128), F32)

    left_t = pf[...]
    left = left_t.T
    left_high, left_low = split(left[:, :ROWS])

    def local_t(b):
        rows = slice(b * RANK, (b + 1) * RANK)
        stacked = jnp.concatenate([left_high[rows], left_low[rows]], axis=0)
        half = width // 2
        for start in range(0, width, 256):
            stop = start + 256
            one = dot(stacked, ch_ref[b, :, start:stop])
            value = one[:RANK] + one[RANK:] + dot(left_high[rows], cl_ref[b, :, start:stop])
            if stop <= half:
                qs[b, 0, :, start:stop] = value
            elif start >= half:
                qs[b, 1, :, start - half : stop - half] = value
            else:
                qs[b, 0, :, start:half] = value[:, : half - start]
                qs[b, 1, :, : stop - half] = value[:, half - start :]

    tiles = width // 2 // 128

    def send_core(b):
        send(qs.at[b, 1 - c], qc.at[b], s1_s.at[b], s1_r.at[b], (x, y, z, 1 - c))

    def send_x(b):
        wait(qc.at[b], s1_r.at[b])
        for t in range(4):
            xs[b, t] = qs[b, c, 8 * t : 8 * t + 8, :] + qc[b, 8 * t : 8 * t + 8, :]
        for i, px in enumerate(x_peers):
            send(xs.at[b, px], xr.at[b, i], s2_s.at[b], s2_r.at[b], (px, y, z, c))

    def send_z(b):
        value = xs[b, x]
        wait(xr.at[b], s2_r.at[b])
        for i in range(NX - 1):
            value = value + xr[b, i]
        for t in range(tiles):
            zs[b, t] = value[:, t * 128 : (t + 1) * 128]
        zs[b, tiles] = jnp.zeros((8, 128), F32)
        for i, pz in enumerate(z_peers):
            send(zs.at[b, pz], zr.at[b, i], s3_s.at[b], s3_r.at[b], (x, y, pz, c))

    def back_z(b):
        value = zs[b, z]
        wait(zr.at[b], s3_r.at[b])
        for i in range(NZ - 1):
            value = value + zr[b, i]
        zg[b, z] = value * (1.0 / 64)
        for pz in z_peers:
            send(zg.at[b, z], zg.at[b, z], s4_s.at[b], s4_r.at[b], (x, y, pz, c))

    def back_x(b):
        wait(zg.at[b, : NZ - 1], s4_r.at[b])
        for t in range(tiles):
            qg[b, c, x, :, t * 128 : (t + 1) * 128] = zg[b, t]
        for px in x_peers:
            send(qg.at[b, c, x], qg.at[b, c, x], s5_s.at[b], s5_r.at[b], (px, y, z, c))

    def send_z_first():
        wait(qc.at[0], s1_r.at[0])
        for t in range(tiles):
            cols = slice(t * 128, (t + 1) * 128)
            fzs[t] = qs[0, c, :, cols] + qc[0, :, cols]
        fzs[tiles] = jnp.zeros((RANK, 128), F32)
        for i, pz in enumerate(z_peers):
            send(fzs.at[pz], fzr.at[i], s2_s.at[0], s2_r.at[0], (x, y, pz, c))

    def send_x_second():
        value = fzs[z]
        wait(fzr, s2_r.at[0])
        for i in range(NZ - 1):
            value = value + fzr[i]
        for t in range(NX):
            fxs[t] = value[8 * t : 8 * t + 8, :]
        for i, px in enumerate(x_peers):
            send(fxs.at[px], fxr.at[i], s3_s.at[0], s3_r.at[0], (px, y, z, c))

    def back_x_second():
        value = fxs[x]
        wait(fxr, s3_r.at[0])
        for i in range(NX - 1):
            value = value + fxr[i]
        fxg[x] = value * (1.0 / 64)
        for px in x_peers:
            send(fxg.at[x], fxg.at[x], s4_s.at[0], s4_r.at[0], (px, y, z, c))

    def back_z_first():
        wait(fxg.at[: NX - 1], s4_r.at[0])
        for t in range(NX):
            fzg[z, 8 * t : 8 * t + 8, :] = fxg[t]
        for pz in z_peers:
            send(fzg.at[z], fzg.at[z], s5_s.at[0], s5_r.at[0], (x, y, pz, c))

    def back_core(b):
        wait(qg.at[b, c, : NX - 1], s5_r.at[b])
        send(qg.at[b, c], qg.at[b, c], s6_s.at[b], s6_r.at[b], (x, y, z, 1 - c))

    for b in range(BUCKETS):
        local_t(b)
        send_core(b)
    send_z_first()
    for b in range(1, BUCKETS):
        send_x(b)
    gram = lax.dot_general(
        left, left_t, (((1,), (0,)), ((), ())), precision=HIGHEST, preferred_element_type=F32
    )
    packed = jnp.zeros((RANK, 128), F32)
    for b in range(BUCKETS):
        packed = jnp.where(lane // RANK == b, gram[b * RANK : (b + 1) * RANK, :], packed)
    done = jnp.zeros((RANK, 128), F32)
    packed, done = eliminate(packed, done, lane, 0, 8)
    packed, done = eliminate(packed, done, lane, 8, 16)
    for b in range(1, BUCKETS):
        send_z(b)
    send_x_second()
    packed, done = eliminate(packed, done, lane, 16, 24)
    packed, done = eliminate(packed, done, lane, 24, 32)
    row = lax.broadcasted_iota(jnp.int32, (RANK, 128), 0)
    inverse = jnp.where(lane % RANK <= row, done, 0.0)
    blocks = [jnp.where(lane // RANK == b, inverse, 0.0) for b in range(BUCKETS)]
    blocks.append(jnp.zeros((RANK, 128), F32))
    factor = jnp.concatenate(blocks, axis=0)
    for b in range(1, BUCKETS):
        back_z(b)
    back_x_second()
    basis_t = lax.dot_general(
        left_t[:ROWS], factor, (((1,), (1,)), ((), ())), precision=HIGHEST, preferred_element_type=F32
    )
    weight_t = lax.dot_general(
        basis_t, factor, (((1,), (0,)), ((), ())), precision=HIGHEST, preferred_element_type=F32
    )
    both = jnp.concatenate([weight_t, inverse], axis=0)
    for b in range(BUCKETS):
        high, low = split(both[:, b * RANK : (b + 1) * RANK])
        w_ref[b] = jnp.concatenate([high, low, high, jnp.zeros_like(high)], axis=1)
    back_z_first()
    for b in range(1, BUCKETS):
        back_x(b)
    wait(pr, pa_s)
    wait(pcs, pc_s)
    wait(zp.at[: NZ - 1], pz_s)
    wait(pg.at[: GROUP - 1], pg_s)
    for b in range(BUCKETS):
        wait(qc.at[b], s1_s.at[b])
        wait(xr.at[b] if b else fzr, s2_s.at[b])
        wait(zr.at[b] if b else fxr, s3_s.at[b])
        wait(zg.at[b, : NZ - 1] if b else fxg.at[: NX - 1], s4_s.at[b])
    for b in range(1, BUCKETS):
        back_core(b)
    wait(fzg.at[: NZ - 1], s5_r.at[0])
    for t in range(tiles):
        for i in range(NX):
            qg[0, c, i, :, t * 128 : (t + 1) * 128] = fzg[t, 8 * i : 8 * i + 8, :]
    send(qg.at[0, c], qg.at[0, c], s6_s.at[0], s6_r.at[0], (x, y, z, 1 - c))
    half = width // 2
    for b in (1, 2, 0):
        wait(qg.at[b, 1 - c], s6_r.at[b])
        for h in range(2):
            cols = slice(h * half, (h + 1) * half)
            high, low = split(jnp.concatenate([qg[b, h, t] for t in range(4)], axis=0))
            stacked = jnp.concatenate([high, high, low, jnp.zeros_like(high)], axis=0)
            both = dot(w_ref[b], stacked)
            q_refs[b][:, cols] = both[ROWS:]
            for i in range(PARTS // BUCKETS):
                rows = slice(i * PART, (i + 1) * PART)
                err_refs[b * (PARTS // BUCKETS) + i][:, cols] = c_ref[b, rows, cols] - both[rows]
    for b in range(BUCKETS):
        wait(qg.at[b, c, : NX - 1] if b else fzg.at[: NZ - 1], s5_s.at[b])
        wait(qg.at[b, c], s6_s.at[b])


def store_kernel(*refs):
    parts, (q_out, err_out, sem) = refs[:-3], refs[-3:]
    copies = []
    for i in range(PARTS):
        b, row = divmod(i * PART, ROWS)
        rows = pl.ds(row, PART)
        copies.append(
            pltpu.make_async_copy(parts[BUCKETS + i], err_out.at[0, b, rows], sem.at[BUCKETS + i])
        )
    for b in range(BUCKETS):
        copies.append(pltpu.make_async_copy(parts[b], q_out.at[b], sem.at[b]))
    for copy in copies:
        copy.start()
    for copy in copies:
        copy.wait()


def per_device(gradient, error_memory, right_factor_initial):
    width = right_factor_initial.shape[2]
    half = width // 2
    dma = pltpu.SemaphoreType.DMA
    vmem = pltpu.VMEM
    whole = pl.BlockSpec(memory_space=pltpu.VMEM)
    hbm = pl.BlockSpec(memory_space=pl.ANY)
    b3 = BUCKETS
    n_xy, n_x, n_z = len(XY), NX - 1, NZ - 1
    made = pl.pallas_call(
        reduce_kernel,
        out_shape=(jax.ShapeDtypeStruct((RANK, width), F32),) * b3
        + (jax.ShapeDtypeStruct((PART, width), F32),) * PARTS,
        in_specs=[hbm] * 3,
        out_specs=(whole,) * (b3 + PARTS),
        scratch_shapes=[
            vmem((b3, ROWS, width), BF16),
            vmem((b3, ROWS, width), F32),
            vmem((b3, RANK, width), F32),
            vmem((b3, ROWS, width), BF16),
            vmem((b3, ROWS, width), BF16),
            vmem((256, width), BF16),
            vmem((b3, ROWS + RANK, 128), BF16),
            vmem((GROUP, PIECE, 128), F32),
            vmem((n_xy, PIECE, 128), F32),
            vmem((PIECE, 128), F32),
            vmem((PIECE, 128), F32),
            vmem((NZ, PIECE, 128), F32),
            vmem((GROUP, PIECE, 128), F32),
            vmem((256, 128), F32),
            vmem((b3, 2, RANK, half), F32),
            vmem((b3, RANK, half), F32),
            vmem((b3, 4, 8, half), F32),
            vmem((b3, n_x, 8, half), F32),
            vmem((b3, NZ, 8, 128), F32),
            vmem((b3, n_z, 8, 128), F32),
            vmem((b3, NZ, 8, 128), F32),
            vmem((b3, 2, 4, 8, half), F32),
            *([dma] * 8),
            *([dma((b3,))] * 12),
            dma((1 + 2 * b3,)),
            vmem((NZ, RANK, 128), F32),
            vmem((n_z, RANK, 128), F32),
            vmem((NX, 8, 128), F32),
            vmem((n_x, 8, 128), F32),
            vmem((NX, 8, 128), F32),
            vmem((NZ, RANK, 128), F32),
        ],
        compiler_params=pltpu.CompilerParams(
            collective_id=0, has_side_effects=True, vmem_limit_bytes=49 << 20
        ),
        name="reduce_kernel",
    )(gradient, error_memory, right_factor_initial)
    return pl.pallas_call(
        store_kernel,
        out_shape=(
            jax.ShapeDtypeStruct((b3, RANK, width), F32),
            jax.ShapeDtypeStruct((1, b3, ROWS, width), F32),
        ),
        in_specs=[hbm] * (b3 + PARTS),
        out_specs=(hbm, hbm),
        scratch_shapes=[dma((b3 + PARTS,))],
        compiler_params=pltpu.CompilerParams(vmem_limit_bytes=1 << 20),
        name="store_kernel",
    )(*made)


def solution(mesh):
    placed = (P("dp", None, None, "mp"), P("dp", None, None, "mp"), P(None, None, "mp"))
    return jax.shard_map(
        per_device,
        mesh=mesh,
        in_specs=placed,
        out_specs=(P(None, None, "mp"), P("dp", None, None, "mp")),
        check_vma=False,
    )
```

```python
import functools

import jax
import jax.numpy as jnp
from jax import lax
from jax.experimental import pallas as pl
from jax.experimental.pallas import tpu as pltpu
from jax.sharding import PartitionSpec as P

MESH = pl.DeviceIdType.MESH
NX, NY, NZ = 4, 4, 8
BUCKETS, RANK, ROWS = 3, 32, 192
GROUP = NX * NY
PIECE = ROWS // GROUP
PARTS = 9
PART = BUCKETS * ROWS // PARTS
HOPS = [0, 1, 2, 1]
XY = sorted(
    ((i, j) for i in range(NX) for j in range(NY) if i or j), key=lambda p: -HOPS[p[0]] - HOPS[p[1]]
)
XS = [2, 1, 3]
ZS = [4, 3, 5, 2, 6, 1, 7]
F32, BF16 = jnp.float32, jnp.bfloat16
HIGHEST = lax.Precision.HIGHEST


def place():
    dp = lax.axis_index("dp")
    return dp // (2 * NZ), lax.axis_index("mp"), (dp // 2) % NZ, dp % 2


def device(x, y, z, c):
    return ((x * NZ + z) * 2 + c, y)


def split(value):
    high = value.astype(BF16)
    return high, (value - high.astype(F32)).astype(BF16)


def dot(a, b, dims=((1,), (0,))):
    return lax.dot_general(a, b, (dims, ((), ())), preferred_element_type=F32)


def eliminate(z, done, lane, start, stop):
    column = lane % RANK
    row = lax.broadcasted_iota(jnp.int32, (RANK, 128), 0)
    group = lane - column
    cols = [jnp.take_along_axis(z, group + k, axis=1) for k in range(start, stop)]
    for t in range(stop - start):
        k = start + t
        scale = lax.rsqrt(cols[t][k : k + 1, :])
        below = jnp.where(row > k, cols[t] * scale, 0.0)
        pivot = jnp.where(column[k : k + 1] == k, scale, z[k : k + 1, :] * scale)
        done = jnp.where(row == k, pivot, done)
        z = jnp.where(column == k, 0.0, z) - below * pivot
        for u in range(t + 1, stop - start):
            cols[u] = cols[u] - below * (cols[u][k : k + 1, :] * scale)
    return z, done


def reduce_kernel(g_hbm, e_hbm, r_hbm, *refs):
    q_refs, err_refs, refs = refs[:BUCKETS], refs[BUCKETS : BUCKETS + PARTS], refs[BUCKETS + PARTS :]
    (
        g_ref, c_ref, r_ref, ch_ref, cl_ref, rr_ref, w_ref,
        ps, pr, pcs, pcr, zp, pg, pf,
        qc, xs, xr, zs, zr, zg, qg,
        pa_s, pa_r, pc_s, pc_r, pz_s, pz_r, pg_s, pg_r,
        s1_s, s1_r, s2_s, s2_r, s3_s, s3_r, s4_s, s4_r, s5_s, s5_r, s6_s, s6_r,
        in_sem, fzs, fzr, fxs, fxr, fxg, fzg,
    ) = refs
    x, y, z, c = place()
    xy_peers = [((x + i) % NX, (y + j) % NY) for i, j in XY]
    x_peers = [(x + i) % NX for i in XS]
    z_peers = [(z + i) % NZ for i in ZS]
    mine = x * NY + y

    loads = [pltpu.make_async_copy(r_hbm, r_ref, in_sem.at[0])]
    for b in range(BUCKETS):
        loads.append(pltpu.make_async_copy(g_hbm.at[0, b], g_ref.at[b], in_sem.at[1 + 2 * b]))
        loads.append(pltpu.make_async_copy(e_hbm.at[0, b], c_ref.at[b], in_sem.at[2 + 2 * b]))
    for load in loads:
        load.start()

    barrier = pltpu.get_barrier_semaphore()
    for px, py in xy_peers:
        pl.semaphore_signal(barrier, inc=1, device_id=device(px, py, z, c), device_id_type=MESH)
    for pz in z_peers:
        pl.semaphore_signal(barrier, inc=1, device_id=device(x, y, pz, c), device_id_type=MESH)
    pl.semaphore_signal(barrier, inc=1, device_id=device(x, y, z, 1 - c), device_id_type=MESH)

    def send(src, dst, send_sem, recv_sem, where):
        pltpu.make_async_remote_copy(
            src_ref=src, dst_ref=dst, send_sem=send_sem, recv_sem=recv_sem,
            device_id=device(*where), device_id_type=MESH,
        ).start()

    def wait(like, sem):
        pltpu.make_async_copy(like, like, sem).wait()

    width = r_ref.shape[2]
    loads[0].wait()
    rr_ref[...] = jnp.zeros_like(rr_ref)
    for b in range(BUCKETS):
        high, low = split(r_ref[b])
        rr_ref[b * RANK : (b + 1) * RANK, :] = high
        rr_ref[128 + b * RANK : 128 + (b + 1) * RANK, :] = low

    lane = lax.broadcasted_iota(jnp.int32, (RANK, 128), 1)
    lane_rows = lax.broadcasted_iota(jnp.int32, (ROWS, 128), 1)
    step = 256
    total = jnp.zeros((ROWS, 128), F32)
    for b in range(BUCKETS):
        loads[1 + 2 * b].wait()
        loads[2 + 2 * b].wait()
        both = jnp.zeros((ROWS, 256), F32)
        rest = jnp.zeros((ROWS, 128), F32)
        for start in range(0, width, step):
            cols = slice(start, start + step)
            value = g_ref[b, :, cols].astype(F32) + c_ref[b, :, cols]
            c_ref[b, :, cols] = value
            high, low = split(value)
            both = both + dot(high, rr_ref[:, cols], ((1,), (1,)))
            rest = rest + dot(low, rr_ref[:128, cols], ((1,), (1,)))
        part = both[:, :128] + both[:, 128:] + rest
        total = jnp.where(lane_rows // RANK == b, part, total)
    total = total * (1.0 / 64)
    for i in range(GROUP):
        ps[i] = total[i * PIECE : (i + 1) * PIECE, :]

    pl.semaphore_wait(barrier, len(XY) + NZ)

    for i, (px, py) in enumerate(xy_peers):
        send(ps.at[px * NY + py], pr.at[i], pa_s, pa_r, (px, py, z, c))
    half = width // 2
    own = pl.ds(pl.multiple_of(c * half, 128), half)
    other = pl.ds(pl.multiple_of((1 - c) * half, 128), half)
    for b in range(BUCKETS):
        send(c_ref.at[b, :, other], qc.at[b], s1_s.at[b], s1_r.at[b], (x, y, z, 1 - c))
    piece = ps[mine]
    wait(pr, pa_r)
    for i in range(len(XY)):
        piece = piece + pr[i]
    pcs[...] = piece
    send(pcs, pcr, pc_s, pc_r, (x, y, z, 1 - c))
    wait(pcr, pc_r)
    zp[z] = piece + pcr[...]
    for pz in z_peers:
        send(zp.at[z], zp.at[z], pz_s, pz_r, (x, y, pz, c))
    for b in range(BUCKETS):
        wait(qc.at[b], s1_r.at[b])

        @pl.loop(0, ROWS // 16)
        def _(i):
            rows = pl.ds(pl.multiple_of(i * 16, 16), 16)
            high, low = split(c_ref[b, rows, own] + qc[b, rows, :])
            ch_ref[b, rows, :] = high
            cl_ref[b, rows, :] = low

    wait(zp.at[: NZ - 1], pz_r)
    piece = zp[0]
    for i in range(1, NZ):
        piece = piece + zp[i]
    pg[mine] = piece
    for px, py in xy_peers:
        send(pg.at[mine], pg.at[mine], pg_s, pg_r, (px, py, z, c))
    wait(pg.at[: GROUP - 1], pg_r)
    for i in range(GROUP):
        pf[i * PIECE : (i + 1) * PIECE, :] = pg[i]
    pf[ROWS:, :] = jnp.zeros((256 - ROWS, 128), F32)

    left_t = pf[...]
    left = left_t.T
    left_high, left_low = split(left[:, :ROWS])

    def local_t(b):
        rows = slice(b * RANK, (b + 1) * RANK)
        stacked = jnp.concatenate([left_high[rows], left_low[rows]], axis=0)
        for start in range(0, half, 256):
            stop = min(start + 256, half)
            one = dot(stacked, ch_ref[b, :, start:stop])
            value = one[:RANK] + one[RANK:] + dot(left_high[rows], cl_ref[b, :, start:stop])
            if b == 0:
                for t in range(start // 128, stop // 128):
                    fzs[t] = value[:, t * 128 - start : t * 128 - start + 128]
            else:
                for t in range(NX):
                    xs[b, t, :, start:stop] = value[8 * t : 8 * t + 8, :]

    tiles = width // 2 // 128

    def send_x(b):
        for i, px in enumerate(x_peers):
            send(xs.at[b, px], xr.at[b, i], s2_s.at[b], s2_r.at[b], (px, y, z, c))

    def send_z(b):
        value = xs[b, x]
        wait(xr.at[b], s2_r.at[b])
        for i in range(NX - 1):
            value = value + xr[b, i]
        for t in range(tiles):
            zs[b, t] = value[:, t * 128 : (t + 1) * 128]
        zs[b, tiles] = jnp.zeros((8, 128), F32)
        for i, pz in enumerate(z_peers):
            send(zs.at[b, pz], zr.at[b, i], s3_s.at[b], s3_r.at[b], (x, y, pz, c))

    def back_z(b):
        value = zs[b, z]
        wait(zr.at[b], s3_r.at[b])
        for i in range(NZ - 1):
            value = value + zr[b, i]
        zg[b, z] = value * (1.0 / 64)
        for pz in z_peers:
            send(zg.at[b, z], zg.at[b, z], s4_s.at[b], s4_r.at[b], (x, y, pz, c))

    def back_x(b):
        wait(zg.at[b, : NZ - 1], s4_r.at[b])
        for t in range(tiles):
            qg[b, c, x, :, t * 128 : (t + 1) * 128] = zg[b, t]
        for px in x_peers:
            send(qg.at[b, c, x], qg.at[b, c, x], s5_s.at[b], s5_r.at[b], (px, y, z, c))

    def send_z_first():
        fzs[tiles] = jnp.zeros((RANK, 128), F32)
        for i, pz in enumerate(z_peers):
            send(fzs.at[pz], fzr.at[i], s2_s.at[0], s2_r.at[0], (x, y, pz, c))

    def send_x_second():
        value = fzs[z]
        wait(fzr, s2_r.at[0])
        for i in range(NZ - 1):
            value = value + fzr[i]
        for t in range(NX):
            fxs[t] = value[8 * t : 8 * t + 8, :]
        for i, px in enumerate(x_peers):
            send(fxs.at[px], fxr.at[i], s3_s.at[0], s3_r.at[0], (px, y, z, c))

    def back_x_second():
        value = fxs[x]
        wait(fxr, s3_r.at[0])
        for i in range(NX - 1):
            value = value + fxr[i]
        fxg[x] = value * (1.0 / 64)
        for px in x_peers:
            send(fxg.at[x], fxg.at[x], s4_s.at[0], s4_r.at[0], (px, y, z, c))

    def back_z_first():
        wait(fxg.at[: NX - 1], s4_r.at[0])
        for t in range(NX):
            fzg[z, 8 * t : 8 * t + 8, :] = fxg[t]
        for pz in z_peers:
            send(fzg.at[z], fzg.at[z], s5_s.at[0], s5_r.at[0], (x, y, pz, c))

    def back_core(b):
        wait(qg.at[b, c, : NX - 1], s5_r.at[b])
        send(qg.at[b, c], qg.at[b, c], s6_s.at[b], s6_r.at[b], (x, y, z, 1 - c))

    local_t(0)
    send_z_first()
    for b in range(1, BUCKETS):
        local_t(b)
        send_x(b)
    gram = lax.dot_general(
        left, left_t, (((1,), (0,)), ((), ())), precision=HIGHEST, preferred_element_type=F32
    )
    packed = jnp.zeros((RANK, 128), F32)
    for b in range(BUCKETS):
        packed = jnp.where(lane // RANK == b, gram[b * RANK : (b + 1) * RANK, :], packed)
    done = jnp.zeros((RANK, 128), F32)
    packed, done = eliminate(packed, done, lane, 0, 8)
    packed, done = eliminate(packed, done, lane, 8, 16)
    for b in range(1, BUCKETS):
        send_z(b)
    send_x_second()
    packed, done = eliminate(packed, done, lane, 16, 24)
    packed, done = eliminate(packed, done, lane, 24, 32)
    row = lax.broadcasted_iota(jnp.int32, (RANK, 128), 0)
    inverse = jnp.where(lane % RANK <= row, done, 0.0)
    blocks = [jnp.where(lane // RANK == b, inverse, 0.0) for b in range(BUCKETS)]
    blocks.append(jnp.zeros((RANK, 128), F32))
    factor = jnp.concatenate(blocks, axis=0)
    for b in range(1, BUCKETS):
        back_z(b)
    back_x_second()
    basis_t = lax.dot_general(
        left_t[:ROWS], factor, (((1,), (1,)), ((), ())), precision=HIGHEST, preferred_element_type=F32
    )
    weight_t = lax.dot_general(
        basis_t, factor, (((1,), (0,)), ((), ())), precision=HIGHEST, preferred_element_type=F32
    )
    both = jnp.concatenate([weight_t, inverse], axis=0)
    for b in range(BUCKETS):
        high, low = split(both[:, b * RANK : (b + 1) * RANK])
        w_ref[b] = jnp.concatenate([high, low, high, jnp.zeros_like(high)], axis=1)
    back_z_first()
    for b in range(1, BUCKETS):
        back_x(b)
    wait(pr, pa_s)
    wait(pcs, pc_s)
    wait(zp.at[: NZ - 1], pz_s)
    wait(pg.at[: GROUP - 1], pg_s)
    for b in range(BUCKETS):
        wait(qc.at[b], s1_s.at[b])
        wait(xr.at[b] if b else fzr, s2_s.at[b])
        wait(zr.at[b] if b else fxr, s3_s.at[b])
        wait(zg.at[b, : NZ - 1] if b else fxg.at[: NX - 1], s4_s.at[b])
    for b in range(1, BUCKETS):
        back_core(b)
    wait(fzg.at[: NZ - 1], s5_r.at[0])
    for t in range(tiles):
        for i in range(NX):
            qg[0, c, i, :, t * 128 : (t + 1) * 128] = fzg[t, 8 * i : 8 * i + 8, :]
    send(qg.at[0, c], qg.at[0, c], s6_s.at[0], s6_r.at[0], (x, y, z, 1 - c))
    half = width // 2
    for b in (1, 2, 0):
        wait(qg.at[b, 1 - c], s6_r.at[b])
        for h in range(2):
            cols = slice(h * half, (h + 1) * half)
            high, low = split(jnp.concatenate([qg[b, h, t] for t in range(4)], axis=0))
            stacked = jnp.concatenate([high, high, low, jnp.zeros_like(high)], axis=0)
            both = dot(w_ref[b], stacked)
            q_refs[b][:, cols] = both[ROWS:]
            for i in range(PARTS // BUCKETS):
                rows = slice(i * PART, (i + 1) * PART)
                err_refs[b * (PARTS // BUCKETS) + i][:, cols] = c_ref[b, rows, cols] - both[rows]
    for b in range(BUCKETS):
        wait(qg.at[b, c, : NX - 1] if b else fzg.at[: NZ - 1], s5_s.at[b])
        wait(qg.at[b, c], s6_s.at[b])


def store_kernel(*refs):
    parts, (q_out, err_out, sem) = refs[:-3], refs[-3:]
    copies = []
    for i in range(PARTS):
        b, row = divmod(i * PART, ROWS)
        rows = pl.ds(row, PART)
        copies.append(
            pltpu.make_async_copy(parts[BUCKETS + i], err_out.at[0, b, rows], sem.at[BUCKETS + i])
        )
    for b in range(BUCKETS):
        copies.append(pltpu.make_async_copy(parts[b], q_out.at[b], sem.at[b]))
    for copy in copies:
        copy.start()
    for copy in copies:
        copy.wait()


def per_device(gradient, error_memory, right_factor_initial):
    width = right_factor_initial.shape[2]
    half = width // 2
    dma = pltpu.SemaphoreType.DMA
    vmem = pltpu.VMEM
    whole = pl.BlockSpec(memory_space=pltpu.VMEM)
    hbm = pl.BlockSpec(memory_space=pl.ANY)
    b3 = BUCKETS
    n_xy, n_x, n_z = len(XY), NX - 1, NZ - 1
    made = pl.pallas_call(
        reduce_kernel,
        out_shape=(jax.ShapeDtypeStruct((RANK, width), F32),) * b3
        + (jax.ShapeDtypeStruct((PART, width), F32),) * PARTS,
        in_specs=[hbm] * 3,
        out_specs=(whole,) * (b3 + PARTS),
        scratch_shapes=[
            vmem((b3, ROWS, width), BF16),
            vmem((b3, ROWS, width), F32),
            vmem((b3, RANK, width), F32),
            vmem((b3, ROWS, half), BF16),
            vmem((b3, ROWS, half), BF16),
            vmem((256, width), BF16),
            vmem((b3, ROWS + RANK, 128), BF16),
            vmem((GROUP, PIECE, 128), F32),
            vmem((n_xy, PIECE, 128), F32),
            vmem((PIECE, 128), F32),
            vmem((PIECE, 128), F32),
            vmem((NZ, PIECE, 128), F32),
            vmem((GROUP, PIECE, 128), F32),
            vmem((256, 128), F32),
            vmem((b3, ROWS, half), F32),
            vmem((b3, 4, 8, half), F32),
            vmem((b3, n_x, 8, half), F32),
            vmem((b3, NZ, 8, 128), F32),
            vmem((b3, n_z, 8, 128), F32),
            vmem((b3, NZ, 8, 128), F32),
            vmem((b3, 2, 4, 8, half), F32),
            *([dma] * 8),
            *([dma((b3,))] * 12),
            dma((1 + 2 * b3,)),
            vmem((NZ, RANK, 128), F32),
            vmem((n_z, RANK, 128), F32),
            vmem((NX, 8, 128), F32),
            vmem((n_x, 8, 128), F32),
            vmem((NX, 8, 128), F32),
            vmem((NZ, RANK, 128), F32),
        ],
        compiler_params=pltpu.CompilerParams(
            collective_id=0, has_side_effects=True, vmem_limit_bytes=49 << 20
        ),
        name="reduce_kernel",
    )(gradient, error_memory, right_factor_initial)
    return pl.pallas_call(
        store_kernel,
        out_shape=(
            jax.ShapeDtypeStruct((b3, RANK, width), F32),
            jax.ShapeDtypeStruct((1, b3, ROWS, width), F32),
        ),
        in_specs=[hbm] * (b3 + PARTS),
        out_specs=(hbm, hbm),
        scratch_shapes=[dma((b3 + PARTS,))],
        compiler_params=pltpu.CompilerParams(vmem_limit_bytes=1 << 20),
        name="store_kernel",
    )(*made)


def solution(mesh):
    placed = (P("dp", None, None, "mp"), P("dp", None, None, "mp"), P(None, None, "mp"))
    return jax.shard_map(
        per_device,
        mesh=mesh,
        in_specs=placed,
        out_specs=(P(None, None, "mp"), P("dp", None, None, "mp")),
        check_vma=False,
    )
```

```python
import functools

import jax
import jax.numpy as jnp
from jax import lax
from jax.experimental import pallas as pl
from jax.experimental.pallas import tpu as pltpu
from jax.sharding import PartitionSpec as P

MESH = pl.DeviceIdType.MESH
NX, NY, NZ = 4, 4, 8
BUCKETS, RANK, ROWS = 3, 32, 192
GROUP = NX * NY
PIECE = ROWS // GROUP
PARTS = 9
PART = BUCKETS * ROWS // PARTS
HOPS = [0, 1, 2, 1]
XY = sorted(
    ((i, j) for i in range(NX) for j in range(NY) if i or j), key=lambda p: -HOPS[p[0]] - HOPS[p[1]]
)
XS = [2, 1, 3]
ZS = [4, 3, 5, 2, 6, 1, 7]
F32, BF16 = jnp.float32, jnp.bfloat16
HIGHEST = lax.Precision.HIGHEST


def place():
    dp = lax.axis_index("dp")
    return dp // (2 * NZ), lax.axis_index("mp"), (dp // 2) % NZ, dp % 2


def device(x, y, z, c):
    return ((x * NZ + z) * 2 + c, y)


def split(value):
    high = value.astype(BF16)
    return high, (value - high.astype(F32)).astype(BF16)


def dot(a, b, dims=((1,), (0,))):
    return lax.dot_general(a, b, (dims, ((), ())), preferred_element_type=F32)


def eliminate(z, done, lane, start, stop):
    column = lane % RANK
    row = lax.broadcasted_iota(jnp.int32, (RANK, 128), 0)
    group = lane - column
    cols = [jnp.take_along_axis(z, group + k, axis=1) for k in range(start, stop)]
    for t in range(stop - start):
        k = start + t
        scale = lax.rsqrt(cols[t][k : k + 1, :])
        below = jnp.where(row > k, cols[t] * scale, 0.0)
        pivot = jnp.where(column[k : k + 1] == k, scale, z[k : k + 1, :] * scale)
        done = jnp.where(row == k, pivot, done)
        z = jnp.where(column == k, 0.0, z) - below * pivot
        for u in range(t + 1, stop - start):
            cols[u] = cols[u] - below * (cols[u][k : k + 1, :] * scale)
    return z, done


def reduce_kernel(g_hbm, e_hbm, r_hbm, *refs):
    q_refs, err_refs, refs = refs[:BUCKETS], refs[BUCKETS : BUCKETS + PARTS], refs[BUCKETS + PARTS :]
    (
        g_ref, c_ref, r_ref, ch_ref, cl_ref, rr_ref, w_ref,
        ps, pr, pcs, pcr, zp, pg, pf,
        qc, xs, xr, zs, zr, zg, qg,
        pa_s, pa_r, pc_r, pz_r, pg_r,
        s1_s, s1_r, s2_s, s2_r, s3_s, s3_r, s4_s, s4_r, s5_s, s5_r, s6_s, s6_r,
        in_sem, like, fzs, fzr, fxs, fxr, fxg, fzg,
    ) = refs
    x, y, z, c = place()
    xy_peers = [((x + i) % NX, (y + j) % NY) for i, j in XY]
    x_peers = [(x + i) % NX for i in XS]
    z_peers = [(z + i) % NZ for i in ZS]
    mine = x * NY + y

    loads = [pltpu.make_async_copy(r_hbm, r_ref, in_sem.at[0])]
    for b in range(BUCKETS):
        loads.append(pltpu.make_async_copy(g_hbm.at[0, b], g_ref.at[b], in_sem.at[1 + 2 * b]))
        loads.append(pltpu.make_async_copy(e_hbm.at[0, b], c_ref.at[b], in_sem.at[2 + 2 * b]))
    for load in loads:
        load.start()

    barrier = pltpu.get_barrier_semaphore()
    for px, py in xy_peers:
        pl.semaphore_signal(barrier, inc=1, device_id=device(px, py, z, c), device_id_type=MESH)
    for pz in z_peers:
        pl.semaphore_signal(barrier, inc=1, device_id=device(x, y, pz, c), device_id_type=MESH)
    pl.semaphore_signal(barrier, inc=1, device_id=device(x, y, z, 1 - c), device_id_type=MESH)

    def send(src, dst, send_sem, recv_sem, where):
        pltpu.make_async_remote_copy(
            src_ref=src, dst_ref=dst, send_sem=send_sem, recv_sem=recv_sem,
            device_id=device(*where), device_id_type=MESH,
        ).start()

    def wait(ref, sem):
        pltpu.make_async_copy(ref, ref, sem).wait()

    width = r_ref.shape[2]
    loads[0].wait()
    rr_ref[...] = jnp.zeros_like(rr_ref)
    for b in range(BUCKETS):
        high, low = split(r_ref[b])
        rr_ref[b * RANK : (b + 1) * RANK, :] = high
        rr_ref[128 + b * RANK : 128 + (b + 1) * RANK, :] = low

    lane = lax.broadcasted_iota(jnp.int32, (RANK, 128), 1)
    lane_rows = lax.broadcasted_iota(jnp.int32, (ROWS, 128), 1)
    step = 256
    total = jnp.zeros((ROWS, 128), F32)
    for b in range(BUCKETS):
        loads[1 + 2 * b].wait()
        loads[2 + 2 * b].wait()
        both = jnp.zeros((ROWS, 256), F32)
        rest = jnp.zeros((ROWS, 128), F32)
        for start in range(0, width, step):
            cols = slice(start, start + step)
            value = g_ref[b, :, cols].astype(F32) + c_ref[b, :, cols]
            c_ref[b, :, cols] = value
            high, low = split(value)
            both = both + dot(high, rr_ref[:, cols], ((1,), (1,)))
            rest = rest + dot(low, rr_ref[:128, cols], ((1,), (1,)))
        part = both[:, :128] + both[:, 128:] + rest
        total = jnp.where(lane_rows // RANK == b, part, total)
    total = total * (1.0 / 64)
    for i in range(GROUP):
        ps[i] = total[i * PIECE : (i + 1) * PIECE, :]

    pl.semaphore_wait(barrier, len(XY) + NZ)

    for i, (px, py) in enumerate(xy_peers):
        send(ps.at[px * NY + py], pr.at[i], pa_s, pa_r, (px, py, z, c))
    half = width // 2
    own = pl.ds(pl.multiple_of(c * half, 128), half)
    other = pl.ds(pl.multiple_of((1 - c) * half, 128), half)
    for b in range(BUCKETS):
        send(c_ref.at[b, :, other], qc.at[b], s1_s, s1_r, (x, y, z, 1 - c))
    piece = ps[mine]
    wait(pr, pa_r)
    for i in range(len(XY)):
        piece = piece + pr[i]
    pcs[...] = piece
    send(pcs, pcr, pa_s, pc_r, (x, y, z, 1 - c))
    wait(pcr, pc_r)
    zp[z] = piece + pcr[...]
    for pz in z_peers:
        send(zp.at[z], zp.at[z], pa_s, pz_r, (x, y, pz, c))
    wait(qc, s1_r)
    for b in range(BUCKETS):

        @pl.loop(0, ROWS // 16)
        def _(i):
            rows = pl.ds(pl.multiple_of(i * 16, 16), 16)
            high, low = split(c_ref[b, rows, own] + qc[b, rows, :])
            ch_ref[b, rows, :] = high
            cl_ref[b, rows, :] = low

    wait(zp.at[: NZ - 1], pz_r)
    piece = zp[0]
    for i in range(1, NZ):
        piece = piece + zp[i]
    pg[mine] = piece
    for px, py in xy_peers:
        send(pg.at[mine], pg.at[mine], pa_s, pg_r, (px, py, z, c))
    wait(pg.at[: GROUP - 1], pg_r)
    for i in range(GROUP):
        pf[i * PIECE : (i + 1) * PIECE, :] = pg[i]
    pf[ROWS:, :] = jnp.zeros((256 - ROWS, 128), F32)

    left_t = pf[...]
    left = left_t.T
    left_high, left_low = split(left[:, :ROWS])

    def local_t(b):
        rows = slice(b * RANK, (b + 1) * RANK)
        stacked = jnp.concatenate([left_high[rows], left_low[rows]], axis=0)
        for start in range(0, half, 256):
            stop = min(start + 256, half)
            one = dot(stacked, ch_ref[b, :, start:stop])
            value = one[:RANK] + one[RANK:] + dot(left_high[rows], cl_ref[b, :, start:stop])
            if b == 0:
                for t in range(start // 128, stop // 128):
                    fzs[t] = value[:, t * 128 - start : t * 128 - start + 128]
            else:
                for t in range(NX):
                    xs[b, t, :, start:stop] = value[8 * t : 8 * t + 8, :]

    tiles = width // 2 // 128

    def send_x(b):
        for i, px in enumerate(x_peers):
            send(xs.at[b, px], xr.at[b, i], s2_s.at[b], s2_r.at[b], (px, y, z, c))

    def send_z(b):
        value = xs[b, x]
        wait(xr.at[b], s2_r.at[b])
        for i in range(NX - 1):
            value = value + xr[b, i]
        for t in range(tiles):
            zs[b, t] = value[:, t * 128 : (t + 1) * 128]
        zs[b, tiles] = jnp.zeros((8, 128), F32)
        for i, pz in enumerate(z_peers):
            send(zs.at[b, pz], zr.at[b, i], s3_s.at[b], s3_r.at[b], (x, y, pz, c))

    def back_z(b):
        value = zs[b, z]
        wait(zr.at[b], s3_r.at[b])
        for i in range(NZ - 1):
            value = value + zr[b, i]
        zg[b, z] = value * (1.0 / 64)
        for pz in z_peers:
            send(zg.at[b, z], zg.at[b, z], s4_s.at[b], s4_r.at[b], (x, y, pz, c))

    def back_x(b):
        wait(zg.at[b, : NZ - 1], s4_r.at[b])
        for t in range(tiles):
            qg[b, c, x, :, t * 128 : (t + 1) * 128] = zg[b, t]
        for px in x_peers:
            send(qg.at[b, c, x], qg.at[b, c, x], s5_s.at[b], s5_r.at[b], (px, y, z, c))

    def send_z_first():
        fzs[tiles] = jnp.zeros((RANK, 128), F32)
        for i, pz in enumerate(z_peers):
            send(fzs.at[pz], fzr.at[i], s2_s.at[0], s2_r.at[0], (x, y, pz, c))

    def send_x_second():
        value = fzs[z]
        wait(fzr, s2_r.at[0])
        for i in range(NZ - 1):
            value = value + fzr[i]
        for t in range(NX):
            fxs[t] = value[8 * t : 8 * t + 8, :]
        for i, px in enumerate(x_peers):
            send(fxs.at[px], fxr.at[i], s3_s.at[0], s3_r.at[0], (px, y, z, c))

    def back_x_second():
        value = fxs[x]
        wait(fxr, s3_r.at[0])
        for i in range(NX - 1):
            value = value + fxr[i]
        fxg[x] = value * (1.0 / 64)
        for px in x_peers:
            send(fxg.at[x], fxg.at[x], s4_s.at[0], s4_r.at[0], (px, y, z, c))

    def back_z_first():
        wait(fxg.at[: NX - 1], s4_r.at[0])
        for t in range(NX):
            fzg[z, 8 * t : 8 * t + 8, :] = fxg[t]
        for pz in z_peers:
            send(fzg.at[z], fzg.at[z], s5_s.at[0], s5_r.at[0], (x, y, pz, c))

    def back_core(b):
        wait(qg.at[b, c, : NX - 1], s5_r.at[b])
        send(qg.at[b, c], qg.at[b, c], s6_s.at[b], s6_r.at[b], (x, y, z, 1 - c))

    local_t(0)
    send_z_first()
    for b in range(1, BUCKETS):
        local_t(b)
        send_x(b)
    gram = lax.dot_general(
        left, left_t, (((1,), (0,)), ((), ())), precision=HIGHEST, preferred_element_type=F32
    )
    packed = jnp.zeros((RANK, 128), F32)
    for b in range(BUCKETS):
        packed = jnp.where(lane // RANK == b, gram[b * RANK : (b + 1) * RANK, :], packed)
    done = jnp.zeros((RANK, 128), F32)
    packed, done = eliminate(packed, done, lane, 0, 8)
    packed, done = eliminate(packed, done, lane, 8, 16)
    for b in range(1, BUCKETS):
        send_z(b)
    send_x_second()
    packed, done = eliminate(packed, done, lane, 16, 24)
    packed, done = eliminate(packed, done, lane, 24, 32)
    row = lax.broadcasted_iota(jnp.int32, (RANK, 128), 0)
    inverse = jnp.where(lane % RANK <= row, done, 0.0)
    blocks = [jnp.where(lane // RANK == b, inverse, 0.0) for b in range(BUCKETS)]
    blocks.append(jnp.zeros((RANK, 128), F32))
    factor = jnp.concatenate(blocks, axis=0)
    for b in range(1, BUCKETS):
        back_z(b)
    back_x_second()
    basis_t = lax.dot_general(
        left_t[:ROWS], factor, (((1,), (1,)), ((), ())), precision=HIGHEST, preferred_element_type=F32
    )
    weight_t = lax.dot_general(
        basis_t, factor, (((1,), (0,)), ((), ())), precision=HIGHEST, preferred_element_type=F32
    )
    both = jnp.concatenate([weight_t, inverse], axis=0)
    for b in range(BUCKETS):
        high, low = split(both[:, b * RANK : (b + 1) * RANK])
        w_ref[b] = jnp.concatenate([high, low, high, jnp.zeros_like(high)], axis=1)
    back_z_first()
    for b in range(1, BUCKETS):
        back_x(b)
    wait(like, pa_s)
    wait(qc, s1_s)
    for b in range(BUCKETS):
        wait(xr.at[b] if b else fzr, s2_s.at[b])
        wait(zr.at[b] if b else fxr, s3_s.at[b])
        wait(zg.at[b, : NZ - 1] if b else fxg.at[: NX - 1], s4_s.at[b])
    for b in range(1, BUCKETS):
        back_core(b)
    wait(fzg.at[: NZ - 1], s5_r.at[0])
    for t in range(tiles):
        for i in range(NX):
            qg[0, c, i, :, t * 128 : (t + 1) * 128] = fzg[t, 8 * i : 8 * i + 8, :]
    send(qg.at[0, c], qg.at[0, c], s6_s.at[0], s6_r.at[0], (x, y, z, 1 - c))
    half = width // 2
    for b in (1, 2, 0):
        wait(qg.at[b, 1 - c], s6_r.at[b])
        for h in range(2):
            cols = slice(h * half, (h + 1) * half)
            high, low = split(jnp.concatenate([qg[b, h, t] for t in range(4)], axis=0))
            stacked = jnp.concatenate([high, high, low, jnp.zeros_like(high)], axis=0)
            both = dot(w_ref[b], stacked)
            q_refs[b][:, cols] = both[ROWS:]
            for i in range(PARTS // BUCKETS):
                rows = slice(i * PART, (i + 1) * PART)
                err_refs[b * (PARTS // BUCKETS) + i][:, cols] = c_ref[b, rows, cols] - both[rows]
    for b in range(BUCKETS):
        wait(qg.at[b, c, : NX - 1] if b else fzg.at[: NZ - 1], s5_s.at[b])
        wait(qg.at[b, c], s6_s.at[b])


def store_kernel(*refs):
    parts, (q_out, err_out, sem) = refs[:-3], refs[-3:]
    copies = []
    for i in range(PARTS):
        b, row = divmod(i * PART, ROWS)
        rows = pl.ds(row, PART)
        copies.append(
            pltpu.make_async_copy(parts[BUCKETS + i], err_out.at[0, b, rows], sem.at[BUCKETS + i])
        )
    for b in range(BUCKETS):
        copies.append(pltpu.make_async_copy(parts[b], q_out.at[b], sem.at[b]))
    for copy in copies:
        copy.start()
    for copy in copies:
        copy.wait()


def per_device(gradient, error_memory, right_factor_initial):
    width = right_factor_initial.shape[2]
    half = width // 2
    dma = pltpu.SemaphoreType.DMA
    vmem = pltpu.VMEM
    whole = pl.BlockSpec(memory_space=pltpu.VMEM)
    hbm = pl.BlockSpec(memory_space=pl.ANY)
    b3 = BUCKETS
    n_xy, n_x, n_z = len(XY), NX - 1, NZ - 1
    made = pl.pallas_call(
        reduce_kernel,
        out_shape=(jax.ShapeDtypeStruct((RANK, width), F32),) * b3
        + (jax.ShapeDtypeStruct((PART, width), F32),) * PARTS,
        in_specs=[hbm] * 3,
        out_specs=(whole,) * (b3 + PARTS),
        scratch_shapes=[
            vmem((b3, ROWS, width), BF16),
            vmem((b3, ROWS, width), F32),
            vmem((b3, RANK, width), F32),
            vmem((b3, ROWS, half), BF16),
            vmem((b3, ROWS, half), BF16),
            vmem((256, width), BF16),
            vmem((b3, ROWS + RANK, 128), BF16),
            vmem((GROUP, PIECE, 128), F32),
            vmem((n_xy, PIECE, 128), F32),
            vmem((PIECE, 128), F32),
            vmem((PIECE, 128), F32),
            vmem((NZ, PIECE, 128), F32),
            vmem((GROUP, PIECE, 128), F32),
            vmem((256, 128), F32),
            vmem((b3, ROWS, half), F32),
            vmem((b3, 4, 8, half), F32),
            vmem((b3, n_x, 8, half), F32),
            vmem((b3, NZ, 8, 128), F32),
            vmem((b3, n_z, 8, 128), F32),
            vmem((b3, NZ, 8, 128), F32),
            vmem((b3, 2, 4, 8, half), F32),
            *([dma] * 7),
            *([dma((b3,))] * 10),
            dma((1 + 2 * b3,)),
            vmem((2 * n_xy + 1 + n_z, PIECE, 128), F32),
            vmem((NZ, RANK, 128), F32),
            vmem((n_z, RANK, 128), F32),
            vmem((NX, 8, 128), F32),
            vmem((n_x, 8, 128), F32),
            vmem((NX, 8, 128), F32),
            vmem((NZ, RANK, 128), F32),
        ],
        compiler_params=pltpu.CompilerParams(
            collective_id=0, has_side_effects=True, vmem_limit_bytes=49 << 20
        ),
        name="reduce_kernel",
    )(gradient, error_memory, right_factor_initial)
    return pl.pallas_call(
        store_kernel,
        out_shape=(
            jax.ShapeDtypeStruct((b3, RANK, width), F32),
            jax.ShapeDtypeStruct((1, b3, ROWS, width), F32),
        ),
        in_specs=[hbm] * (b3 + PARTS),
        out_specs=(hbm, hbm),
        scratch_shapes=[dma((b3 + PARTS,))],
        compiler_params=pltpu.CompilerParams(vmem_limit_bytes=1 << 20),
        name="store_kernel",
    )(*made)


def solution(mesh):
    placed = (P("dp", None, None, "mp"), P("dp", None, None, "mp"), P(None, None, "mp"))
    return jax.shard_map(
        per_device,
        mesh=mesh,
        in_specs=placed,
        out_specs=(P(None, None, "mp"), P("dp", None, None, "mp")),
        check_vma=False,
    )
```
